512 devices in a mesh: group: 4 (over x), dp: 32 (over y_lo, z, core), fsdp: 4 (over y_hi).
Axes of the slice: x: 4, y: 8 (y_hi: 4, y_lo: 2; y = y_hi * 2 + y_lo), z: 8, core: 2. Of those that a mesh axis runs over, the one named last changes fastest.
Arguments:
- student_tokens: bfloat16 [65536, 1280], P(('group', 'dp', 'fsdp')), may hold values from -6 to 6
- sam_maps: bfloat16 [4, 16384, 256], P(None, ('dp', 'fsdp'), 'group'), may hold values from -8 to 8
- dino_maps: bfloat16 [4, 16384, 1536], P(None, ('dp', 'fsdp'), 'group'), may hold values from -8 to 8
- sam_gain: float32 [256], replicated, may hold values from 0.1 to 1.9
- dino_gain: float32 [1536], replicated, may hold values from 0.1 to 1.9
- patch_counts: int32 [64], replicated, may hold values from 256 to 1024
- sam_in: bfloat16 [1280, 1280], P(('dp', 'fsdp')), may hold values from -0.15625 to 0.15625
- sam_out: bfloat16 [1280, 256], P(('dp', 'fsdp')), may hold values from -1 to 1
- dino_in: bfloat16 [1280, 1280], P(('dp', 'fsdp')), may hold values from -0.15625 to 0.15625
- dino_out: bfloat16 [1280, 1536], P(('dp', 'fsdp')), may hold values from -1 to 1
Outputs:
- token_grad: bfloat16 [65536, 1280], P(('group', 'dp', 'fsdp'))
- loss: float32 [], replicated
The draws below stay inside these ranges and needn't reach their ends.
All inputs are finite; a program needn't handle non-finite values.
Results may differ from the reference program's by a relative error of at most 0.018.
Values may be sent and summed in bfloat16 or wider, within the bound.
No kernel may reach another device: no remote copies, remote signals or barrier semaphores. Data moves between devices by JAX's collectives and lax.ppermute only.
A program may use at most 64 MiB of HBM per device.

```python
import math
import jax
import jax.numpy as jnp
from jax import lax

D = 1280
HID = 1280
CS = 256
CD = 1536
IMG_TOK = 1024
TOKENS = 65536
IMAGES = 64
N_GROUP = 4


def out_weight(key, salt, rows, cols):
    values = jax.random.normal(jax.random.fold_in(key, salt), (rows, cols), jnp.float32)
    return jnp.clip(values, -6.0, 6.0) / math.sqrt(rows)


def teacher_features(key, weights, noise, low, high):
    chans = weights.shape[1]
    direction = jnp.sum(weights, axis=0)
    strength = jnp.exp(jax.random.uniform(key, (IMAGES,), jnp.float32, math.log(low), math.log(high)))
    token_strength = jnp.repeat(strength, IMG_TOK)
    values = token_strength[:, None] * direction[None, :] + noise
    return jnp.clip(values, -8.0, 8.0).reshape(N_GROUP, TOKENS // N_GROUP, chans).astype(jnp.bfloat16)


def draw_sam_out(key, part):
    weights = out_weight(key, 101, HID, CS)
    return weights.astype(jnp.bfloat16)


def draw_dino_out(key, part):
    weights = out_weight(key, 202, HID, CD)
    return weights.astype(jnp.bfloat16)


def draw_sam_maps(key, part):
    weights = out_weight(key, 101, HID, CS)
    key = jax.random.fold_in(key, 5)
    noise = jax.random.normal(jax.random.fold_in(key, 1), (TOKENS, CS), jnp.float32)
    low_end = 0.12
    return teacher_features(jax.random.fold_in(key, 2), weights, noise, low_end, 2.5)


def draw_dino_maps(key, part):
    weights = out_weight(key, 202, HID, CD)
    key = jax.random.fold_in(key, 6)
    noise = jax.random.normal(jax.random.fold_in(key, 1), (TOKENS, CD), jnp.float32)
    low_end = 0.12
    return teacher_features(jax.random.fold_in(key, 2), weights, noise, low_end, 2.5)


def place_ends(entries, own_key, least, largest):
    spot = [jax.random.randint(jax.random.fold_in(own_key, axis), (), 0, length) for axis, length in enumerate(entries.shape)]
    main_axis = entries.shape.index(max(entries.shape))
    next_to = spot[:main_axis] + [(spot[main_axis] + 1) % entries.shape[main_axis]] + spot[main_axis + 1:]
    return entries.at[tuple(spot)].set(least).at[tuple(next_to)].set(largest)


def level_of(rng, extent, split, low, largest):
    def one(axis_at, parts):
        draws = jax.random.uniform(jax.random.fold_in(jax.random.fold_in(rng, 6), axis_at), (parts,), jnp.float32, low / len(split), largest / len(split))
        return jnp.repeat(jnp.exp(draws), extent[axis_at] // parts).reshape((-1,) + (1,) * (len(extent) - axis_at - 1))

    loudness = one(*split[0])
    for cut in split[1:]:
        loudness = loudness * one(*cut)
    return loudness


def scatter_about(key, shape, width, most, pieces=(), held_as=jnp.bfloat16):
    result = width * jax.random.normal(key, shape, jnp.float32)
    if pieces:
        result = result * level_of(key, shape, pieces, -0.22, 0.18)
    return jnp.clip(result, -most, most).astype(held_as)


def setup_inputs(seed: int = 0) -> dict:
    seeds = jax.random.split(jax.random.key(seed), 11)
    return {
        "student_tokens": scatter_about(seeds[0], (TOKENS, D), 1.0, 6.0, ((0, 512),)),
        "sam_maps": draw_sam_maps(jax.random.fold_in(seeds[10], 71), 0),
        "dino_maps": draw_dino_maps(jax.random.fold_in(seeds[10], 71), 0),
        "sam_gain": jnp.clip(1.0 + 0.18 * jax.random.normal(seeds[3], (CS,), jnp.float32), 0.1, 1.9),
        "dino_gain": jnp.clip(1.0 + 0.18 * jax.random.normal(seeds[4], (CD,), jnp.float32), 0.1, 1.9),
        "patch_counts": place_ends(jax.random.randint(seeds[5], (IMAGES,), IMG_TOK // 4, IMG_TOK + 1), jax.random.fold_in(seeds[5], 1), IMG_TOK // 4, IMG_TOK).astype(jnp.int32),
        "sam_in": scatter_about(seeds[6], (D, HID), D ** -0.5, 0.15625, ((0, 128),)),
        "sam_out": draw_sam_out(jax.random.fold_in(seeds[10], 71), 0),
        "dino_in": scatter_about(seeds[8], (D, HID), D ** -0.5, 0.15625, ((0, 128),)),
        "dino_out": draw_dino_out(jax.random.fold_in(seeds[10], 71), 0),
    }


def teacher_targets(features, gain):
    values = features.astype(jnp.float32)
    center = lax.optimization_barrier(jnp.mean(values, axis=-1, keepdims=True))
    spread = lax.optimization_barrier(jnp.mean(values * values, axis=-1, keepdims=True)) - center * center
    return ((values - center) * lax.rsqrt(spread + 1e-06) * gain).astype(jnp.bfloat16)

def head_forward(tokens, w_first, w_second, target):
    pre = jnp.dot(tokens, w_first, preferred_element_type=jnp.float32)
    act = jax.nn.gelu(pre).astype(jnp.bfloat16)
    pred = jnp.dot(act, w_second, preferred_element_type=jnp.float32)
    goal = target.astype(jnp.float32)
    pp_mean = lax.optimization_barrier(jnp.mean(pred * pred, axis=-1)) + 1e-05
    tt_mean = lax.optimization_barrier(jnp.mean(goal * goal, axis=-1)) + 1e-05
    pt_mean = lax.optimization_barrier(jnp.mean(pred * goal, axis=-1))
    inv_root = lax.rsqrt(pp_mean * tt_mean)
    cosine = pt_mean * inv_root
    return (pre, pred, goal, pp_mean, inv_root, cosine)

def head_backward(pre, pred, goal, pp_mean, inv_root, cosine, weight_row, w_first, w_second):
    chans = pred.shape[1]
    back = -weight_row[:, None] * (goal * inv_root[:, None] - (cosine / pp_mean)[:, None] * pred) / chans
    back = back.astype(jnp.bfloat16)
    hid_back = jnp.dot(back, w_second.T, preferred_element_type=jnp.float32)
    hid_back = jax.vjp(jax.nn.gelu, pre)[1](hid_back)[0].astype(jnp.bfloat16)
    return jnp.dot(hid_back, w_first.T, preferred_element_type=jnp.float32)

def reference(student_tokens, sam_maps, dino_maps, sam_gain, dino_gain, patch_counts, sam_in, sam_out, dino_in, dino_out):
    target_s = teacher_targets(sam_maps.reshape(TOKENS, CS), sam_gain)
    target_d = teacher_targets(dino_maps.reshape(TOKENS, CD), dino_gain)
    position = jnp.arange(TOKENS, dtype=jnp.int32)
    image = position // IMG_TOK
    live = (position % IMG_TOK < patch_counts[image]).astype(jnp.float32)
    count = jnp.sum(live)
    blocks = TOKENS // IMG_TOK

    def one_block(items):
        tokens, goal_s, goal_d, live_b = items
        fwd_s = head_forward(tokens, sam_in, sam_out, goal_s)
        fwd_d = head_forward(tokens, dino_in, dino_out, goal_d)
        loss_part = jnp.sum(live_b * (2.0 - fwd_s[5] - fwd_d[5]))
        scale = live_b / count
        grad = head_backward(*fwd_s, scale, sam_in, sam_out) + head_backward(*fwd_d, scale, dino_in, dino_out)
        return (loss_part, grad.astype(jnp.bfloat16))
    loss_parts, grads = lax.map(one_block, (student_tokens.reshape(blocks, IMG_TOK, D), target_s.reshape(blocks, IMG_TOK, CS), target_d.reshape(blocks, IMG_TOK, CD), live.reshape(blocks, IMG_TOK)))
    return (grads.reshape(TOKENS, D), jnp.sum(loss_parts) / count)
```

```python
import jax
import jax.numpy as jnp
from jax import lax
from jax.sharding import Mesh, PartitionSpec as P

IMG_TOK = 1024
AXES = ("x", "ylo", "z", "core", "yhi")
PLANE = ("ylo", "z", "yhi")
IN_Q = 640
DINO_Q = 384
SAM_Q = 64
PAD_Q = 64


def ring(n, shift):
    return [(i, (i + shift) % n) for i in range(n)]


def quarter_of(q, w_in, dino_out, sam_out):
    rows = w_in.shape[0]
    part_in = lax.dynamic_slice(w_in, (0, q * IN_Q), (rows, IN_Q))
    part_d = lax.dynamic_slice(dino_out, (0, q * DINO_Q), (rows, DINO_Q))
    sam = sam_out.reshape(rows, 4, SAM_Q)
    part_s = lax.dynamic_index_in_dim(sam, q, axis=1, keepdims=False)
    pad = jnp.zeros((rows, PAD_Q), w_in.dtype)
    return jnp.concatenate([part_in, part_d, part_s, pad], axis=1)


def gather_plane(part):
    rows, cols = part.shape
    part = part.reshape(1, rows // 2, 2, cols)
    many = jnp.broadcast_to(part, (64, rows // 2, 2, cols))
    return lax.all_to_all(many, PLANE, split_axis=0, concat_axis=0, tiled=True)


def swap_core(value):
    return lax.ppermute(value, "core", ring(2, 1))


def natural_rows(mine, other, core):
    first = jnp.where(core == 0, mine, other)
    second = jnp.where(core == 0, other, mine)
    cols = mine.shape[-1]
    both = jnp.stack([first.reshape(16, 4, 5, 2, cols), second.reshape(16, 4, 5, 2, cols)], axis=1)
    return both.reshape(1280, cols)


def shards(
    student_tokens,
    sam_maps,
    dino_maps,
    sam_gain,
    dino_gain,
    patch_counts,
    sam_in,
    sam_out,
    dino_in,
    dino_out,
):
    rows = student_tokens.shape[0]
    x = lax.axis_index("x")
    core = lax.axis_index("core")
    f32 = jnp.float32
    bf16 = jnp.bfloat16

    def dot(a, b):
        return jnp.dot(a, b, preferred_element_type=f32)

    w_in = jnp.concatenate([sam_in, dino_in], axis=1)
    own_g = gather_plane(quarter_of(x, w_in, dino_out, sam_out))
    opp_part = quarter_of((x + 2) % 4, w_in, dino_out, sam_out)
    own_g, opp_part = lax.optimization_barrier((own_g, opp_part))
    opp_g = gather_plane(opp_part)

    feats = jnp.concatenate([dino_maps, sam_maps], axis=2)

    def feat_for(slot):
        return lax.dynamic_index_in_dim(feats, (x - slot) % 4, axis=0, keepdims=False)

    got = [feat_for(0)] + [lax.ppermute(feat_for(s), "x", ring(4, -s)) for s in (1, 2, 3)]

    own_full = natural_rows(own_g, swap_core(own_g), core)
    half = IN_Q

    def halves(full):
        mine = lax.dynamic_slice(full, (core * half, 0), (half, full.shape[1]))
        other = lax.dynamic_slice(full, ((1 - core) * half, 0), (half, full.shape[1]))
        return mine, other

    own = halves(own_full)
    next_m = lax.ppermute(own[0], "x", ring(4, -1))
    prev_m = lax.ppermute(own[0], "x", ring(4, 1))
    next_o = swap_core(next_m)
    prev_o = swap_core(prev_m)
    opp_full = natural_rows(opp_g, swap_core(opp_g), core)
    opp = halves(opp_full)
    slots = [own, (next_m, next_o), opp, (prev_m, prev_o)]

    feat = [g.astype(f32) for g in got]
    gains_d = dino_gain.reshape(4, DINO_Q)
    gains_s = sam_gain.reshape(4, SAM_Q)

    def targets(parts, gains):
        chans = 4 * parts[0].shape[1]
        center = sum(jnp.sum(p, axis=1, keepdims=True) for p in parts) / chans
        spread = sum(jnp.sum(p * p, axis=1, keepdims=True) for p in parts) / chans - center * center
        root = lax.rsqrt(spread + 1e-06)
        out = []
        for j, p in enumerate(parts):
            gain = lax.dynamic_index_in_dim(gains, (x + j) % 4, axis=0, keepdims=True)
            out.append(((p - center) * root * gain).astype(bf16).astype(f32))
        return out

    goal_d = targets([f[:, :DINO_Q] for f in feat], gains_d)
    goal_s = targets([f[:, DINO_Q:] for f in feat], gains_s)

    tok_m = lax.dynamic_slice(student_tokens, (0, core * half), (rows, half))
    tok_o = lax.dynamic_slice(student_tokens, (0, (1 - core) * half), (rows, half))
    pre_slots = jnp.stack([dot(tok_m, m[:, :IN_Q]) + dot(tok_o, o[:, :IN_Q]) for m, o in slots])
    pre = [lax.dynamic_index_in_dim(pre_slots, (q - x) % 4, axis=0, keepdims=False) for q in range(4)]
    act = jnp.stack([jax.nn.gelu(p).astype(bf16) for p in pre])

    def act_of(head, h):
        return lax.dynamic_index_in_dim(act, 2 * head + h, axis=0, keepdims=False)

    def preds(head, lo, hi):
        am, ao = act_of(head, core), act_of(head, 1 - core)
        return [dot(am, m[:, lo:hi]) + dot(ao, o[:, lo:hi]) for m, o in slots]

    s_cols = (IN_Q + DINO_Q, IN_Q + DINO_Q + SAM_Q)
    d_cols = (IN_Q, IN_Q + DINO_Q)
    pred_s = preds(0, *s_cols)
    pred_d = preds(1, *d_cols)

    def scores(pred, goal):
        chans = 4 * pred[0].shape[1]
        pp = sum(jnp.sum(p * p, axis=1, keepdims=True) for p in pred) / chans + 1e-05
        tt = sum(jnp.sum(g * g, axis=1, keepdims=True) for g in goal) / chans + 1e-05
        pt = sum(jnp.sum(p * g, axis=1, keepdims=True) for p, g in zip(pred, goal)) / chans
        inv_root = lax.rsqrt(pp * tt)
        return pp, inv_root, pt * inv_root

    sc_s = scores(pred_s, goal_s)
    sc_d = scores(pred_d, goal_d)

    start = lax.axis_index(AXES) * rows
    image = start // IMG_TOK
    limit = lax.dynamic_index_in_dim(patch_counts, image, keepdims=False)
    slot_at = start % IMG_TOK + jnp.arange(rows, dtype=jnp.int32)
    live = (slot_at < limit).astype(f32)[:, None]
    count = jnp.sum(jnp.clip(patch_counts, 0, IMG_TOK)).astype(f32)

    local = jnp.sum(live * (2.0 - sc_s[2] - sc_d[2]))
    local = lax.psum(local, "core")
    local = lax.psum(local, "x")
    spread_out = jnp.broadcast_to(local, (64, 1, 128))
    all_parts = lax.all_to_all(spread_out, PLANE, split_axis=0, concat_axis=0, tiled=True)
    loss = jnp.sum(all_parts[:, 0, 0]) / count

    scale = live / count

    def backs(pred, goal, score):
        pp, inv_root, cosine = score
        chans = 4 * pred[0].shape[1]
        return [
            (-scale * (g * inv_root - (cosine / pp) * p) / chans).astype(bf16)
            for p, g in zip(pred, goal)
        ]

    back_s = backs(pred_s, goal_s, sc_s)
    back_d = backs(pred_d, goal_d, sc_d)

    def hid_backs(back, lo, hi):
        m = sum(dot(b, w[0][:, lo:hi].T) for b, w in zip(back, slots))
        o = sum(dot(b, w[1][:, lo:hi].T) for b, w in zip(back, slots))
        return jnp.where(core == 0, m, o), jnp.where(core == 0, o, m)

    hid = [*hid_backs(back_s, *s_cols), *hid_backs(back_d, *d_cols)]
    hid = jnp.stack([jax.vjp(jax.nn.gelu, p)[1](h)[0].astype(bf16) for p, h in zip(pre, hid)])
    grad_m = jnp.zeros((rows, half), f32)
    grad_o = jnp.zeros((rows, half), f32)
    for j, (m, o) in enumerate(slots):
        h = lax.dynamic_index_in_dim(hid, (x + j) % 4, axis=0, keepdims=False)
        grad_m += dot(h, m[:, :IN_Q].T)
        grad_o += dot(h, o[:, :IN_Q].T)
    first = jnp.where(core == 0, grad_m, grad_o)
    second = jnp.where(core == 0, grad_o, grad_m)
    grad = jnp.concatenate([first, second], axis=1).astype(bf16)
    return (grad, loss)


def solution(mesh):
    fine = Mesh(mesh.devices.reshape(4, 2, 8, 2, 4), AXES)
    tokens = P(AXES, None)
    rest = ("ylo", "z", "core", "yhi")
    return jax.shard_map(
        shards,
        mesh=fine,
        in_specs=(
            tokens,
            P(None, rest, "x"),
            P(None, rest, "x"),
            P(),
            P(),
            P(),
            P(rest, None),
            P(rest, None),
            P(rest, None),
            P(rest, None),
        ),
        out_specs=(tokens, P()),
        check_vma=False,
    )
```

```python
import functools

import jax
import jax.numpy as jnp
from jax import lax
from jax.experimental import pallas as pl
from jax.experimental.pallas import tpu as pltpu
from jax.sharding import Mesh, PartitionSpec as P

IMG_TOK = 1024
AXES = ("x", "ylo", "z", "core", "yhi")
PLANE = ("ylo", "z", "yhi")
HALF = 640
DINO_Q = 384
SAM_Q = 64
OUT_Q = 512
COLS = HALF + OUT_Q
S_AT = HALF + DINO_Q
F32 = jnp.float32
BF16 = jnp.bfloat16
VMEM_LIMIT = 56 * 1024 * 1024


def ring(n, shift):
    return [(i, (i + shift) % n) for i in range(n)]


def dot(a, b):
    return jnp.dot(a, b, preferred_element_type=F32)


def dot_t(a, b):
    return lax.dot_general(a, b, (((1,), (1,)), ((), ())), preferred_element_type=F32)


def pick_cols(half):
    source = lax.broadcasted_iota(jnp.int32, (2 * HALF, HALF), 0)
    at = lax.broadcasted_iota(jnp.int32, (2 * HALF, HALF), 1)
    return (source == (at // 40) * 80 + half * 40 + at % 40).astype(BF16)


def gelu_slope(v):
    c = 0.7978845608028654
    t = jnp.tanh(c * (v + 0.044715 * (v * v * v)))
    return 0.5 * (1.0 + t) + 0.5 * v * (1.0 - t * t) * (c * (1.0 + 3.0 * 0.044715 * (v * v)))


def forward_kernel(
    where, tok_m, tok_o, pre0, pre1, pre3, goal, tt, live,
    m0, o0, m1, o1, m2, o2, m3, o3,
    pred, pre2, score, part, act,
):
    x, core = where[0], where[1]
    pre2[...] = dot(tok_m[...], m2[:, :HALF]) + dot(tok_o[...], o2[:, :HALF])
    for j, ref in enumerate((pre0, pre1, pre2, pre3)):
        act[lax.rem(x + j, 4)] = jax.nn.gelu(ref[...]).astype(BF16)
    sm, so = act[core], act[1 - core]
    dm, do = act[2 + core], act[3 - core]
    slots = ((m0, o0), (m1, o1), (m2, o2), (m3, o3))
    pp = [0.0, 0.0]
    pt = [0.0, 0.0]
    for j, (m, o) in enumerate(slots):
        for head, (am, ao, lo, hi) in enumerate(((sm, so, DINO_Q, OUT_Q), (dm, do, 0, DINO_Q))):
            value = dot(am, m[:, HALF + lo:HALF + hi]) + dot(ao, o[:, HALF + lo:HALF + hi])
            pred[j, :, lo:hi] = value
            aim = goal[j, :, lo:hi].astype(F32)
            pp[head] += jnp.sum(value * value, axis=1, keepdims=True)
            pt[head] += jnp.sum(value * aim, axis=1, keepdims=True)
    total = 0.0
    for head, chans in enumerate((4 * SAM_Q, 4 * DINO_Q)):
        mean = pp[head] / chans + 1e-05
        inv_root = lax.rsqrt(mean * tt[:, head:head + 1])
        cosine = pt[head] / chans * inv_root
        score[:, 2 * head:2 * head + 1] = inv_root
        score[:, 2 * head + 1:2 * head + 2] = cosine / mean
        total += cosine
    part[...] = jnp.sum(live[...] * (2.0 - total), axis=0, keepdims=True) + jnp.zeros((1, 128), F32)


def backward_kernel(
    where, pred, goal, score, scale, pre0, pre1, pre2, pre3,
    m0, o0, m1, o1, m2, o2, m3, o3,
    grad, pre, hid,
):
    x, core = where[0], where[1]
    for j, ref in enumerate((pre0, pre1, pre2, pre3)):
        pre[lax.rem(x + j, 4)] = ref[...]
    slots = ((m0, o0), (m1, o1), (m2, o2), (m3, o3))
    sums = [[0.0, 0.0], [0.0, 0.0]]
    for j, (m, o) in enumerate(slots):
        for head, (lo, hi, chans) in enumerate(((DINO_Q, OUT_Q, 4 * SAM_Q), (0, DINO_Q, 4 * DINO_Q))):
            aim = goal[j, :, lo:hi].astype(F32)
            inv_root = score[:, 2 * head:2 * head + 1]
            ratio = score[:, 2 * head + 1:2 * head + 2]
            back = (-scale[...] * (aim * inv_root - ratio * pred[j, :, lo:hi]) / chans).astype(BF16)
            sums[head][0] += dot_t(back, m[:, HALF + lo:HALF + hi])
            sums[head][1] += dot_t(back, o[:, HALF + lo:HALF + hi])
    for head in range(2):
        for side in range(2):
            at = 2 * head + (core if side == 0 else 1 - core)
            hid[at] = (sums[head][side] * gelu_slope(pre[at])).astype(BF16)
    for side in range(2):
        total = 0.0
        for j, pair in enumerate(slots):
            total += dot_t(hid[lax.rem(x + j, 4)], pair[side][:, :HALF])
        grad[core if side == 0 else 1 - core] = total.astype(BF16)


def shards(
    student_tokens,
    sam_maps,
    dino_maps,
    sam_gain,
    dino_gain,
    patch_counts,
    sam_in,
    sam_out,
    dino_in,
    dino_out,
):
    rows = student_tokens.shape[0]
    x = lax.axis_index("x")
    core = lax.axis_index("core")
    shard = sam_in.shape[0]

    both = jnp.concatenate([sam_in, dino_in], axis=0)
    picked = dot(both, pick_cols(x % 2)).astype(BF16).reshape(2, shard, HALF)
    sam4 = sam_out.reshape(shard, 4, SAM_Q)

    def payload(q):
        part_in = lax.dynamic_index_in_dim(picked, q // 2, axis=0, keepdims=False)
        part_d = lax.dynamic_slice(dino_out, (0, q * DINO_Q), (shard, DINO_Q))
        part_s = lax.dynamic_index_in_dim(sam4, q, axis=1, keepdims=False)
        pad = jnp.zeros((shard, COLS - S_AT - SAM_Q), BF16)
        part = jnp.concatenate([part_in, part_d, part_s, pad], axis=1)
        return jnp.broadcast_to(part.reshape(1, shard // 2, 2, COLS), (64, shard // 2, 2, COLS))

    def gather_plane(many):
        got = lax.all_to_all(many, PLANE, split_axis=0, concat_axis=0, tiled=True)
        return got

    own_b, opp_b, feats = lax.optimization_barrier(
        (payload(x), payload((x + 2) % 4), jnp.concatenate(
            [dino_maps, sam_maps, jnp.zeros((4, rows, OUT_Q - DINO_Q - SAM_Q), BF16)], axis=2)))

    def feat_for(slot):
        return lax.dynamic_index_in_dim(feats, (x - slot) % 4, axis=0, keepdims=False)

    got = [feat_for(0)] + [lax.ppermute(feat_for(s), "x", ring(4, -s)) for s in (1, 2, 3)]
    tok_m = dot(student_tokens, pick_cols(core)).astype(BF16)
    tok_o = dot(student_tokens, pick_cols(1 - core)).astype(BF16)

    own_g = gather_plane(own_b)
    own_g, got, tok_m, tok_o = lax.optimization_barrier((own_g, got, tok_m, tok_o))
    opp_b, own_g = lax.optimization_barrier((opp_b, own_g))
    opp_g = gather_plane(opp_b)

    own = own_g.reshape(HALF, COLS)
    next_m = lax.ppermute(own, "x", ring(4, -1))
    prev_m = lax.ppermute(own, "x", ring(4, 1))

    def swap(value):
        return lax.ppermute(value, "core", ring(2, 1))

    opp = opp_g.reshape(HALF, COLS)
    slots = [(w, swap(w)) for w in (own, next_m, opp, prev_m)]

    def gain_of(slot):
        q = (x + slot) % 4
        d = lax.dynamic_slice(dino_gain, (q * DINO_Q,), (DINO_Q,))
        s = lax.dynamic_slice(sam_gain, (q * SAM_Q,), (SAM_Q,))
        return jnp.concatenate([d, s, jnp.zeros((OUT_Q - DINO_Q - SAM_Q,), F32)])

    feat = jnp.stack(got).astype(F32)
    gain = jnp.stack([gain_of(j) for j in range(4)])[:, None, :]

    def targets(part, weight):
        chans = 4 * (DINO_Q if part.shape[2] == DINO_Q else SAM_Q)
        center = jnp.sum(part, axis=(0, 2), keepdims=True) / chans
        spread = jnp.sum(part * part, axis=(0, 2), keepdims=True) / chans - center * center
        value = ((part - center) * lax.rsqrt(spread + 1e-06) * weight).astype(BF16)
        wide = value.astype(F32)
        return value, jnp.sum(wide * wide, axis=(0, 2))[:, None] / chans + 1e-05

    goal_d, tt_d = targets(feat[:, :, :DINO_Q], gain[:, :, :DINO_Q])
    goal_s, tt_s = targets(feat[:, :, DINO_Q:], gain[:, :, DINO_Q:])
    goal = jnp.concatenate([goal_d, goal_s], axis=2)
    tt = jnp.concatenate([tt_s, tt_d], axis=1)

    start = lax.axis_index(AXES) * rows
    limit = lax.dynamic_index_in_dim(patch_counts, start // IMG_TOK, keepdims=False)
    slot_at = start % IMG_TOK + jnp.arange(rows, dtype=jnp.int32)
    live = (slot_at < limit).astype(F32)[:, None]
    count = jnp.sum(jnp.clip(patch_counts, 0, IMG_TOK)).astype(F32)

    pre = {j: dot(tok_m, slots[j][0][:, :HALF]) + dot(tok_o, slots[j][1][:, :HALF]) for j in (0, 1, 3)}
    goal, tt, live, pre = lax.optimization_barrier((goal, tt, live, pre))
    place = jnp.stack([x, core]).astype(jnp.int32)
    flat = [w for pair in slots for w in pair]
    in_vmem = pl.BlockSpec(memory_space=pltpu.VMEM)
    in_smem = pl.BlockSpec(memory_space=pltpu.SMEM)
    pred, pre2, score, part = pl.pallas_call(
        forward_kernel,
        out_shape=(
            jax.ShapeDtypeStruct((4, rows, OUT_Q), F32),
            jax.ShapeDtypeStruct((rows, HALF), F32),
            jax.ShapeDtypeStruct((rows, 4), F32),
            jax.ShapeDtypeStruct((1, 128), F32),
        ),
        in_specs=[in_smem] + [in_vmem] * 16,
        out_specs=(in_vmem,) * 4,
        scratch_shapes=[pltpu.VMEM((4, rows, HALF), BF16)],
        compiler_params=pltpu.CompilerParams(vmem_limit_bytes=VMEM_LIMIT),
        name="forward",
    )(place, tok_m, tok_o, pre[0], pre[1], pre[3], goal, tt, live, *flat)

    local = lax.psum(lax.psum(part[0, 0], "core"), "x")
    spread_out = jnp.broadcast_to(local, (64, 1, 128))
    all_parts = lax.all_to_all(spread_out, PLANE, split_axis=0, concat_axis=0, tiled=True)
    loss = jnp.sum(all_parts[:, 0, 0]) / count

    grad = pl.pallas_call(
        backward_kernel,
        out_shape=jax.ShapeDtypeStruct((2, rows, HALF), BF16),
        in_specs=[in_smem] + [in_vmem] * 16,
        out_specs=in_vmem,
        scratch_shapes=[pltpu.VMEM((4, rows, HALF), F32), pltpu.VMEM((4, rows, HALF), BF16)],
        compiler_params=pltpu.CompilerParams(vmem_limit_bytes=VMEM_LIMIT),
        name="backward",
    )(place, pred, goal, score, live / count, pre[0], pre[1], pre2, pre[3], *flat)
    grad = dot_t(grad[0], pick_cols(0)) + dot_t(grad[1], pick_cols(1))
    return (grad.astype(BF16), loss)


def solution(mesh):
    fine = Mesh(mesh.devices.reshape(4, 2, 8, 2, 4), AXES)
    tokens = P(AXES, None)
    rest = ("ylo", "z", "core", "yhi")
    return jax.shard_map(
        shards,
        mesh=fine,
        in_specs=(
            tokens,
            P(None, rest, "x"),
            P(None, rest, "x"),
            P(),
            P(),
            P(),
            P(rest, None),
            P(rest, None),
            P(rest, None),
            P(rest, None),
        ),
        out_specs=(tokens, P()),
        check_vma=False,
    )
```

```python
import functools

import jax
import jax.numpy as jnp
from jax import lax
from jax.experimental import pallas as pl
from jax.experimental.pallas import tpu as pltpu
from jax.sharding import Mesh, PartitionSpec as P

IMG_TOK = 1024
AXES = ("x", "ylo", "z", "core", "yhi")
PLANE = ("ylo", "z", "yhi")
HALF = 640
DINO_Q = 384
SAM_Q = 64
OUT_Q = 512
COLS = HALF + OUT_Q
S_AT = HALF + DINO_Q
F32 = jnp.float32
BF16 = jnp.bfloat16
VMEM_LIMIT = 56 * 1024 * 1024


def ring(n, shift):
    return [(i, (i + shift) % n) for i in range(n)]


def dot(a, b):
    return jnp.dot(a, b, preferred_element_type=F32)


def dot_t(a, b):
    return lax.dot_general(a, b, (((1,), (1,)), ((), ())), preferred_element_type=F32)


def pick_cols(half):
    source = lax.broadcasted_iota(jnp.int32, (2 * HALF, HALF), 0)
    at = lax.broadcasted_iota(jnp.int32, (2 * HALF, HALF), 1)
    return (source == (at // 40) * 80 + half * 40 + at % 40).astype(BF16)


def gelu_slope(v):
    c = 0.7978845608028654
    t = jnp.tanh(c * (v + 0.044715 * (v * v * v)))
    return 0.5 * (1.0 + t) + 0.5 * v * (1.0 - t * t) * (c * (1.0 + 3.0 * 0.044715 * (v * v)))


def copies(refs, lo, hi, buf, sems, first=0):
    return [
        pltpu.make_async_copy(ref.at[:, pl.ds(lo, hi - lo)], buf.at[i], sems.at[first + i])
        for i, ref in enumerate(refs)
    ]


def forward_kernel(
    where, tok_o, pre0, half1, half2, half3, goal, tt, live,
    m0, o0, m1, o1, m2, o2, m3, o3,
    pred, pre, score, part, act, w_in, w_out, sems,
):
    x, core = where[0], where[1]
    got_in = copies((o1, o3, o2), 0, HALF, w_in, sems)
    got_out = copies((m0, o0, m1, o1, m3, o3, m2, o2), HALF, COLS, w_out, sems, 3)
    for copy in got_in + got_out:
        copy.start()
    for i, (j, ref) in enumerate(((0, pre0), (1, half1), (3, half3), (2, half2))):
        value = ref[...]
        if i > 0:
            got_in[i - 1].wait()
            value += dot(tok_o[...], w_in[i - 1])
        at = lax.rem(x + j, 4)
        pre[at] = value
        act[at] = jax.nn.gelu(value).astype(BF16)
    sm, so = act[core], act[1 - core]
    dm, do = act[2 + core], act[3 - core]
    pp = [0.0, 0.0]
    pt = [0.0, 0.0]
    for i, j in enumerate((0, 1, 3, 2)):
        got_out[2 * i].wait()
        got_out[2 * i + 1].wait()
        for head, (am, ao, lo, hi) in enumerate(((sm, so, DINO_Q, OUT_Q), (dm, do, 0, DINO_Q))):
            value = dot(am, w_out[2 * i, :, lo:hi]) + dot(ao, w_out[2 * i + 1, :, lo:hi])
            pred[j, :, lo:hi] = value
            aim = goal[j, :, lo:hi].astype(F32)
            pp[head] += jnp.sum(value * value, axis=1, keepdims=True)
            pt[head] += jnp.sum(value * aim, axis=1, keepdims=True)
    total = 0.0
    for head, chans in enumerate((4 * SAM_Q, 4 * DINO_Q)):
        mean = pp[head] / chans + 1e-05
        inv_root = lax.rsqrt(mean * tt[:, head:head + 1])
        cosine = pt[head] / chans * inv_root
        score[:, 2 * head:2 * head + 1] = inv_root
        score[:, 2 * head + 1:2 * head + 2] = cosine / mean
        total += cosine
    loss = jnp.sum(live[...] * (2.0 - total), axis=0, keepdims=True)
    part[...] = loss[:, :, None] + jnp.zeros(part.shape, F32)


def hidden_kernel(
    where, pred, goal, score, scale, pre,
    m0, o0, m1, o1, m2, o2, m3, o3,
    hid, w_out, sems,
):
    core = where[1]
    got = copies((m0, o0, m1, o1, m2, o2, m3, o3), HALF, COLS, w_out, sems)
    for copy in got:
        copy.start()
    sums = [[0.0, 0.0], [0.0, 0.0]]
    for j in range(4):
        got[2 * j].wait()
        got[2 * j + 1].wait()
        for head, (lo, hi, chans) in enumerate(((DINO_Q, OUT_Q, 4 * SAM_Q), (0, DINO_Q, 4 * DINO_Q))):
            aim = goal[j, :, lo:hi].astype(F32)
            inv_root = score[:, 2 * head:2 * head + 1]
            ratio = score[:, 2 * head + 1:2 * head + 2]
            back = (-scale[...] * (aim * inv_root - ratio * pred[j, :, lo:hi]) / chans).astype(BF16)
            sums[head][0] += dot_t(back, w_out[2 * j, :, lo:hi])
            sums[head][1] += dot_t(back, w_out[2 * j + 1, :, lo:hi])
    for head in range(2):
        for side in range(2):
            at = 2 * head + (core if side == 0 else 1 - core)
            hid[at] = (sums[head][side] * gelu_slope(pre[at])).astype(BF16)


def grad_kernel(where, hid, m0, o0, m1, o1, m2, o2, m3, o3, grad, w_in, sems):
    x, core = where[0], where[1]
    got = copies((m0, o0, m1, o1, m2, o2, m3, o3), 0, HALF, w_in, sems)
    for copy in got:
        copy.start()
    total = [0.0, 0.0]
    for j in range(4):
        h = hid[lax.rem(x + j, 4)]
        for side in range(2):
            got[2 * j + side].wait()
            total[side] += dot_t(h, w_in[2 * j + side])
    grad[core] = total[0].astype(BF16)
    grad[1 - core] = total[1].astype(BF16)


def shards(
    student_tokens,
    sam_maps,
    dino_maps,
    sam_gain,
    dino_gain,
    patch_counts,
    sam_in,
    sam_out,
    dino_in,
    dino_out,
):
    rows = student_tokens.shape[0]
    x = lax.axis_index("x")
    core = lax.axis_index("core")
    shard = sam_in.shape[0]

    both = jnp.concatenate([sam_in, dino_in], axis=0)
    picked = dot(both, pick_cols(x % 2)).astype(BF16).reshape(2, shard, HALF)
    sam4 = sam_out.reshape(shard, 4, SAM_Q)

    def payload(q):
        part_in = lax.dynamic_index_in_dim(picked, q // 2, axis=0, keepdims=False)
        part_d = lax.dynamic_slice(dino_out, (0, q * DINO_Q), (shard, DINO_Q))
        part_s = lax.dynamic_index_in_dim(sam4, q, axis=1, keepdims=False)
        pad = jnp.zeros((shard, COLS - S_AT - SAM_Q), BF16)
        part = jnp.concatenate([part_in, part_d, part_s, pad], axis=1)
        return jnp.broadcast_to(part.reshape(1, shard // 2, 2, COLS), (64, shard // 2, 2, COLS))

    def gather_plane(many):
        got = lax.all_to_all(many, PLANE, split_axis=0, concat_axis=0, tiled=True)
        return got

    own_b = payload(x)
    opp_b, dino_maps, sam_maps = lax.optimization_barrier((payload((x + 2) % 4), dino_maps, sam_maps))
    feats = jnp.concatenate(
        [dino_maps, sam_maps, jnp.zeros((4, rows, OUT_Q - DINO_Q - SAM_Q), BF16)], axis=2)

    def feat_for(slot):
        return lax.dynamic_index_in_dim(feats, (x - slot) % 4, axis=0, keepdims=False)

    got = [feat_for(0)] + [lax.ppermute(feat_for(s), "x", ring(4, -s)) for s in (1, 2, 3)]
    tok_m = dot(student_tokens, pick_cols(core)).astype(BF16)
    tok_o = dot(student_tokens, pick_cols(1 - core)).astype(BF16)

    own_g = gather_plane(own_b)
    own_g, opp_b, got, tok_m, tok_o = lax.optimization_barrier((own_g, opp_b, got, tok_m, tok_o))
    opp_g = gather_plane(opp_b)

    def swap(value):
        return lax.ppermute(value, "core", ring(2, 1))

    def gain_of(slot):
        q = (x + slot) % 4
        d = lax.dynamic_slice(dino_gain, (q * DINO_Q,), (DINO_Q,))
        s = lax.dynamic_slice(sam_gain, (q * SAM_Q,), (SAM_Q,))
        return jnp.concatenate([d, s, jnp.zeros((OUT_Q - DINO_Q - SAM_Q,), F32)])

    feat = jnp.stack(got).astype(F32)
    gain = jnp.stack([gain_of(j) for j in range(4)])[:, None, :]

    def targets(part, weight):
        chans = 4 * (DINO_Q if part.shape[2] == DINO_Q else SAM_Q)
        center = jnp.sum(part, axis=(0, 2), keepdims=True) / chans
        spread = jnp.sum(part * part, axis=(0, 2), keepdims=True) / chans - center * center
        value = ((part - center) * lax.rsqrt(spread + 1e-06) * weight).astype(BF16)
        wide = value.astype(F32)
        return value, jnp.sum(wide * wide, axis=(0, 2))[:, None] / chans + 1e-05

    goal_d, tt_d = targets(feat[:, :, :DINO_Q], gain[:, :, :DINO_Q])
    goal_s, tt_s = targets(feat[:, :, DINO_Q:], gain[:, :, DINO_Q:])
    goal = jnp.concatenate([goal_d, goal_s], axis=2)
    tt = jnp.concatenate([tt_s, tt_d], axis=1)

    start = lax.axis_index(AXES) * rows
    limit = lax.dynamic_index_in_dim(patch_counts, start // IMG_TOK, keepdims=False)
    slot_at = start % IMG_TOK + jnp.arange(rows, dtype=jnp.int32)
    live = (slot_at < limit).astype(F32)[:, None]
    count = jnp.sum(jnp.clip(patch_counts, 0, IMG_TOK)).astype(F32)

    place = jnp.stack([x, core]).astype(jnp.int32)
    scale = live / count
    own = own_g.reshape(HALF, COLS)
    next_m = lax.ppermute(own, "x", ring(4, -1))
    prev_m = lax.ppermute(own, "x", ring(4, 1))
    opp = opp_g.reshape(HALF, COLS)
    pre0 = dot(tok_m, own[:, :HALF])
    own, pre0 = lax.optimization_barrier((own, pre0))
    own_o = swap(own)
    pre0 += dot(tok_o, own_o[:, :HALF])
    next_m, prev_m, opp, pre0, goal, tt, live, scale, place = lax.optimization_barrier(
        (next_m, prev_m, opp, pre0, goal, tt, live, scale, place))
    slots = [(own, own_o)] + [(w, swap(w)) for w in (next_m, opp, prev_m)]

    part = [dot(tok_m, w[:, :HALF]) for w in (next_m, opp, prev_m)]
    flat = [w for pair in slots for w in pair]
    in_vmem = pl.BlockSpec(memory_space=pltpu.VMEM)
    anywhere = pl.BlockSpec(memory_space=pl.ANY)
    in_smem = pl.BlockSpec(memory_space=pltpu.SMEM)
    params = pltpu.CompilerParams(vmem_limit_bytes=VMEM_LIMIT)
    pred, pre, score, loss = pl.pallas_call(
        forward_kernel,
        out_shape=(
            jax.ShapeDtypeStruct((4, rows, OUT_Q), F32),
            jax.ShapeDtypeStruct((4, rows, HALF), F32),
            jax.ShapeDtypeStruct((rows, 4), F32),
            jax.ShapeDtypeStruct((8, 1, 128), F32),
        ),
        in_specs=[in_smem] + [in_vmem] * 8 + [anywhere] * 8,
        out_specs=(in_vmem,) * 4,
        scratch_shapes=[
            pltpu.VMEM((4, rows, HALF), BF16),
            pltpu.VMEM((3, HALF, HALF), BF16),
            pltpu.VMEM((8, HALF, OUT_Q), BF16),
            pltpu.SemaphoreType.DMA((11,)),
        ],
        compiler_params=params,
        name="forward",
    )(place, tok_o, pre0, *part, goal, tt, live, *flat)

    loss = lax.all_to_all(loss, ("x", "core"), split_axis=0, concat_axis=0, tiled=True)
    hid = pl.pallas_call(
        hidden_kernel,
        out_shape=jax.ShapeDtypeStruct((4, rows, HALF), BF16),
        in_specs=[in_smem] + [in_vmem] * 5 + [anywhere] * 8,
        out_specs=in_vmem,
        scratch_shapes=[pltpu.VMEM((8, HALF, OUT_Q), BF16), pltpu.SemaphoreType.DMA((8,))],
        compiler_params=params,
        name="hidden",
    )(place, pred, goal, score, scale, pre, *flat)

    loss = jnp.broadcast_to(jnp.sum(loss, axis=0, keepdims=True), (64, 1, 128))
    loss, hid = lax.optimization_barrier((loss, hid))
    loss = lax.all_to_all(loss, PLANE, split_axis=0, concat_axis=0, tiled=True)
    loss = jnp.sum(loss[:, 0, 0]) / count

    grad = pl.pallas_call(
        grad_kernel,
        out_shape=jax.ShapeDtypeStruct((2, rows, HALF), BF16),
        in_specs=[in_smem, in_vmem] + [anywhere] * 8,
        out_specs=in_vmem,
        scratch_shapes=[pltpu.VMEM((8, HALF, HALF), BF16), pltpu.SemaphoreType.DMA((8,))],
        compiler_params=params,
        name="grad",
    )(place, hid, *flat)
    grad = dot_t(grad[0], pick_cols(0)) + dot_t(grad[1], pick_cols(1))
    return (grad.astype(BF16), loss)


def solution(mesh):
    fine = Mesh(mesh.devices.reshape(4, 2, 8, 2, 4), AXES)
    tokens = P(AXES, None)
    rest = ("ylo", "z", "core", "yhi")
    return jax.shard_map(
        shards,
        mesh=fine,
        in_specs=(
            tokens,
            P(None, rest, "x"),
            P(None, rest, "x"),
            P(),
            P(),
            P(),
            P(rest, None),
            P(rest, None),
            P(rest, None),
            P(rest, None),
        ),
        out_specs=(tokens, P()),
        check_vma=False,
    )
```

```python
import functools

import jax
import jax.numpy as jnp
from jax import lax
from jax.experimental import pallas as pl
from jax.experimental.pallas import tpu as pltpu
from jax.sharding import Mesh, PartitionSpec as P

IMG_TOK = 1024
AXES = ("x", "ylo", "z", "core", "yhi")
PLANE = ("ylo", "z", "yhi")
HALF = 640
DINO_Q = 384
SAM_Q = 64
SAM = 256
FEAT_Q = 512
FAR = 256
COLS = HALF + DINO_Q
OPP_COLS = COLS - FAR + SAM
F32 = jnp.float32
BF16 = jnp.bfloat16
VMEM_LIMIT = 56 * 1024 * 1024


def ring(n, shift):
    return [(i, (i + shift) % n) for i in range(n)]


def dot(a, b):
    return jnp.dot(a, b, preferred_element_type=F32)


def dot_t(a, b):
    return lax.dot_general(a, b, (((1,), (1,)), ((), ())), preferred_element_type=F32)


def pick_cols(half):
    source = lax.broadcasted_iota(jnp.int32, (2 * HALF, HALF), 0)
    at = lax.broadcasted_iota(jnp.int32, (2 * HALF, HALF), 1)
    return (source == (at // 40) * 80 + half * 40 + at % 40).astype(BF16)


def gelu_slope(v):
    c = 0.7978845608028654
    t = jnp.tanh(c * (v + 0.044715 * (v * v * v)))
    return 0.5 * (1.0 + t) + 0.5 * v * (1.0 - t * t) * (c * (1.0 + 3.0 * 0.044715 * (v * v)))


def copies(refs, lo, hi, buf, sems, first=0):
    return [
        pltpu.make_async_copy(ref.at[:, pl.ds(lo, hi - lo)], buf.at[i], sems.at[first + i])
        for i, ref in enumerate(refs)
    ]


def far_copies(opp, far, buf, at, sems, first):
    low, high = pl.ds(0, FAR), pl.ds(FAR, DINO_Q - FAR)
    out = []
    for i, (a, b) in enumerate(zip(opp, far)):
        out.append(pltpu.make_async_copy(b, buf.at[at + i, :, low], sems.at[first + 2 * i]))
        source = a.at[:, pl.ds(HALF, DINO_Q - FAR)]
        out.append(pltpu.make_async_copy(source, buf.at[at + i, :, high], sems.at[first + 2 * i + 1]))
    return out


def forward_kernel(
    where, tok_m, tok_o, pre0, goal_s, goal_d, live,
    m0, o0, m1, o1, m2, o2, m3, o3, mf, of,
    pred_s, pred_d, pre, score, part, act, w_in, w_out, w_sam, sems,
):
    x, core = where[0], where[1]
    got_in = copies((m1, o1, m3, o3, m2, o2), 0, HALF, w_in, sems)
    got_out = copies((m0, o0, m1, o1, m3, o3), HALF, COLS, w_out, sems, 6)
    got_far = far_copies((m2, o2), (mf, of), w_out, 6, sems, 12)
    got_sam = copies((m2, o2), OPP_COLS - SAM, OPP_COLS, w_sam, sems, 16)
    for copy in got_in + got_out + got_far + got_sam:
        copy.start()
    for i, j in enumerate((0, 1, 3, 2)):
        if i == 0:
            value = pre0[...]
        else:
            got_in[2 * i - 2].wait()
            got_in[2 * i - 1].wait()
            value = dot(tok_m[...], w_in[2 * i - 2]) + dot(tok_o[...], w_in[2 * i - 1])
        at = lax.rem(x + j, 4)
        pre[at] = value
        act[at] = jax.nn.gelu(value).astype(BF16)

    def sums(value, aim):
        return [jnp.sum(v, axis=1, keepdims=True) for v in (value * value, aim * aim, value * aim)]

    found = [0.0, 0.0, 0.0]
    dm, do = act[2 + core], act[3 - core]
    for i, j in enumerate((0, 1, 3, 2)):
        for copy in got_out[2 * i:2 * i + 2] or got_far:
            copy.wait()
        value = dot(dm, w_out[2 * i]) + dot(do, w_out[2 * i + 1])
        pred_d[j] = value
        found = [a + b for a, b in zip(found, sums(value, goal_d[j].astype(F32)))]
    for copy in got_sam:
        copy.wait()
    value = dot(act[core], w_sam[0]) + dot(act[1 - core], w_sam[1])
    pred_s[...] = value
    total = 0.0
    heads = ((SAM, sums(value, goal_s[...].astype(F32))), (4 * DINO_Q, found))
    for head, (chans, (pp, tt, pt)) in enumerate(heads):
        mean = pp / chans + 1e-05
        inv_root = lax.rsqrt(mean * (tt / chans + 1e-05))
        cosine = pt / chans * inv_root
        score[:, 2 * head:2 * head + 1] = inv_root
        score[:, 2 * head + 1:2 * head + 2] = cosine / mean
        total += cosine
    loss = jnp.sum(live[...] * (2.0 - total), axis=0, keepdims=True)
    part[...] = loss[:, :, None] + jnp.zeros(part.shape, F32)


def hidden_kernel(
    where, pred_s, pred_d, goal_s, goal_d, score, scale, pre,
    m0, o0, m1, o1, m2, o2, m3, o3, mf, of,
    hid, w_out, w_sam, sems,
):
    core = where[1]
    got_sam = copies((m2, o2), OPP_COLS - SAM, OPP_COLS, w_sam, sems)
    got_out = copies((m0, o0, m1, o1, m3, o3), HALF, COLS, w_out, sems, 2)
    got_far = far_copies((m2, o2), (mf, of), w_out, 6, sems, 8)
    for copy in got_sam + got_out + got_far:
        copy.start()

    def back(head, pred, goal, chans):
        inv_root = score[:, 2 * head:2 * head + 1]
        ratio = score[:, 2 * head + 1:2 * head + 2]
        return (-scale[...] * (goal.astype(F32) * inv_root - ratio * pred) / chans).astype(BF16)

    def finish(head, found):
        for side, value in enumerate(found):
            at = 2 * head + (core if side == 0 else 1 - core)
            hid[at] = (value * gelu_slope(pre[at])).astype(BF16)

    value = back(0, pred_s[...], goal_s[...], SAM)
    for copy in got_sam:
        copy.wait()
    finish(0, [dot_t(value, w_sam[side]) for side in range(2)])
    found = [0.0, 0.0]
    for i, j in enumerate((0, 1, 3, 2)):
        value = back(1, pred_d[j], goal_d[j], 4 * DINO_Q)
        for copy in got_out[2 * i:2 * i + 2] or got_far:
            copy.wait()
        for side in range(2):
            found[side] += dot_t(value, w_out[2 * i + side])
    finish(1, found)


def grad_kernel(where, hid, m0, o0, m1, o1, m2, o2, m3, o3, grad, w_in, sems):
    x, core = where[0], where[1]
    got = copies((m0, o0, m1, o1, m2, o2, m3, o3), 0, HALF, w_in, sems)
    for copy in got:
        copy.start()
    total = [0.0, 0.0]
    for j in range(4):
        h = hid[lax.rem(x + j, 4)]
        for side in range(2):
            got[2 * j + side].wait()
            total[side] += dot_t(h, w_in[2 * j + side])
    at = lax.broadcasted_iota(jnp.int32, (1, HALF), 1)
    block = (at * 1639) >> 16
    row = lax.broadcasted_iota(jnp.int32, (2 * HALF, HALF), 0)
    whole = 0.0
    for side, half in enumerate((core, 1 - core)):
        source = at + block * 40 + half * 40
        whole += dot_t(total[side].astype(BF16), (row == source).astype(BF16))
    grad[...] = whole.astype(BF16)


def shards(
    student_tokens,
    sam_maps,
    dino_maps,
    sam_gain,
    dino_gain,
    patch_counts,
    sam_in,
    sam_out,
    dino_in,
    dino_out,
):
    rows = student_tokens.shape[0]
    x = lax.axis_index("x")
    core = lax.axis_index("core")
    shard = sam_in.shape[0]

    both = jnp.concatenate([sam_in, dino_in], axis=0)
    picked = dot(both, pick_cols(x % 2)).astype(BF16).reshape(2, shard, HALF)

    def payload(q, first, extra):
        part_in = lax.dynamic_index_in_dim(picked, q // 2, axis=0, keepdims=False)
        part_d = lax.dynamic_slice(dino_out, (0, q * DINO_Q + first), (shard, DINO_Q - first))
        part = jnp.concatenate([part_in, part_d] + extra, axis=1)
        cols = part.shape[1]
        return jnp.broadcast_to(part.reshape(1, shard // 2, 2, cols), (64, shard // 2, 2, cols))

    def gather_plane(many):
        return lax.all_to_all(many, PLANE, split_axis=0, concat_axis=0, tiled=True)

    own_b = payload(x, 0, [])
    sam4 = sam_out.reshape(shard, 4, SAM_Q)
    sam_parts = [lax.dynamic_index_in_dim(sam4, (x + j) % 4, axis=1, keepdims=False) for j in range(4)]
    opp_b, dino_maps, sam_maps = lax.optimization_barrier(
        (payload((x + 2) % 4, FAR, sam_parts), dino_maps, sam_maps))
    feats = jnp.concatenate(
        [dino_maps, sam_maps, jnp.zeros((4, rows, FEAT_Q - DINO_Q - SAM_Q), BF16)], axis=2)

    def feat_for(slot):
        return lax.dynamic_index_in_dim(feats, (x - slot) % 4, axis=0, keepdims=False)

    got = [feat_for(0)] + [lax.ppermute(feat_for(s), "x", ring(4, -s)) for s in (1, 2, 3)]
    tok_m = dot(student_tokens, pick_cols(core)).astype(BF16)
    tok_o = dot(student_tokens, pick_cols(1 - core)).astype(BF16)

    own_g = gather_plane(own_b)
    start = lax.axis_index(AXES) * rows
    limit = lax.dynamic_index_in_dim(patch_counts, start // IMG_TOK, keepdims=False)
    slot_at = start % IMG_TOK + jnp.arange(rows, dtype=jnp.int32)
    live = (slot_at < limit).astype(F32)[:, None]
    count = jnp.sum(jnp.clip(patch_counts, 0, IMG_TOK)).astype(F32)

    place = jnp.stack([x, core]).astype(jnp.int32)
    scale = live / count
    own, opp_b, got, tok_m, tok_o, live, scale, place = lax.optimization_barrier(
        (own_g.reshape(HALF, COLS), opp_b, got, tok_m, tok_o, live, scale, place))
    opp_g = gather_plane(opp_b)

    def swap(value):
        return lax.ppermute(value, "core", ring(2, 1))

    def gains(gain, width):
        return [lax.dynamic_slice(gain, ((x + j) % 4 * width,), (width,)) for j in range(4)]

    def targets(part, gain):
        chans = 4 * part.shape[2] if part.shape[0] == 4 else part.shape[2]
        center = jnp.sum(part, axis=(0, 2), keepdims=True) / chans
        spread = jnp.sum(part * part, axis=(0, 2), keepdims=True) / chans - center * center
        return ((part - center) * lax.rsqrt(spread + 1e-06) * gain).astype(BF16)

    next_m = lax.ppermute(own, "x", ring(4, -1))
    prev_m = lax.ppermute(own, "x", ring(4, 1))
    far_m = lax.ppermute(own[:, HALF:HALF + FAR], "x", ring(4, 2))
    pre0 = dot(tok_m, own[:, :HALF])
    own, pre0 = lax.optimization_barrier((own, pre0))
    own_o = swap(own)
    own_o, got = lax.optimization_barrier((own_o, got))
    pre0 += dot(tok_o, own_o[:, :HALF])
    feat_d = jnp.stack([g[:, :DINO_Q] for g in got]).astype(F32)
    feat_s = jnp.concatenate([g[:, DINO_Q:DINO_Q + SAM_Q] for g in got], axis=1).astype(F32)
    goal_d = targets(feat_d, jnp.stack(gains(dino_gain, DINO_Q))[:, None, :])
    goal_s = targets(feat_s[None], jnp.concatenate(gains(sam_gain, SAM_Q))[None, None, :])[0]

    next_m, prev_m, far_m, pre0, goal_s, goal_d = lax.optimization_barrier(
        (next_m, prev_m, far_m, pre0, goal_s, goal_d))
    next_o, prev_o, far_o = swap(next_m), swap(prev_m), swap(far_m)
    opp = opp_g.reshape(HALF, OPP_COLS)
    slots = [(own, own_o), (next_m, next_o), (opp, swap(opp)), (prev_m, prev_o)]
    flat = [w for pair in slots for w in pair]
    in_vmem = pl.BlockSpec(memory_space=pltpu.VMEM)
    anywhere = pl.BlockSpec(memory_space=pl.ANY)
    in_smem = pl.BlockSpec(memory_space=pltpu.SMEM)
    params = pltpu.CompilerParams(vmem_limit_bytes=VMEM_LIMIT)
    pred_s, pred_d, pre, score, loss = pl.pallas_call(
        forward_kernel,
        out_shape=(
            jax.ShapeDtypeStruct((rows, SAM), F32),
            jax.ShapeDtypeStruct((4, rows, DINO_Q), F32),
            jax.ShapeDtypeStruct((4, rows, HALF), F32),
            jax.ShapeDtypeStruct((rows, 4), F32),
            jax.ShapeDtypeStruct((16, 1, 128), F32),
        ),
        in_specs=[in_smem] + [in_vmem] * 6 + [anywhere] * 10,
        out_specs=(in_vmem,) * 5,
        scratch_shapes=[
            pltpu.VMEM((4, rows, HALF), BF16),
            pltpu.VMEM((6, HALF, HALF), BF16),
            pltpu.VMEM((8, HALF, DINO_Q), BF16),
            pltpu.VMEM((2, HALF, SAM), BF16),
            pltpu.SemaphoreType.DMA((18,)),
        ],
        compiler_params=params,
        name="forward",
    )(place, tok_m, tok_o, pre0, goal_s, goal_d, live, *flat, far_m, far_o)

    loss = lax.all_to_all(loss, ("x", "ylo", "core"), split_axis=0, concat_axis=0, tiled=True)
    hid = pl.pallas_call(
        hidden_kernel,
        out_shape=jax.ShapeDtypeStruct((4, rows, HALF), BF16),
        in_specs=[in_smem] + [in_vmem] * 7 + [anywhere] * 10,
        out_specs=in_vmem,
        scratch_shapes=[
            pltpu.VMEM((8, HALF, DINO_Q), BF16),
            pltpu.VMEM((2, HALF, SAM), BF16),
            pltpu.SemaphoreType.DMA((12,)),
        ],
        compiler_params=params,
        name="hidden",
    )(place, pred_s, pred_d, goal_s, goal_d, score, scale, pre, *flat, far_m, far_o)

    loss = jnp.broadcast_to(jnp.sum(loss, axis=0, keepdims=True), (32, 1, 128))
    loss, hid = lax.optimization_barrier((loss, hid))
    loss = lax.all_to_all(loss, ("z", "yhi"), split_axis=0, concat_axis=0, tiled=True)
    loss = jnp.sum(loss[:, 0, 0]) / count

    grad = pl.pallas_call(
        grad_kernel,
        out_shape=jax.ShapeDtypeStruct((rows, 2 * HALF), BF16),
        in_specs=[in_smem, in_vmem] + [anywhere] * 8,
        out_specs=in_vmem,
        scratch_shapes=[pltpu.VMEM((8, HALF, HALF), BF16), pltpu.SemaphoreType.DMA((8,))],
        compiler_params=params,
        name="grad",
    )(place, hid, *flat)
    return (grad, loss)


def solution(mesh):
    fine = Mesh(mesh.devices.reshape(4, 2, 8, 2, 4), AXES)
    tokens = P(AXES, None)
    rest = ("ylo", "z", "core", "yhi")
    return jax.shard_map(
        shards,
        mesh=fine,
        in_specs=(
            tokens,
            P(None, rest, "x"),
            P(None, rest, "x"),
            P(),
            P(),
            P(),
            P(rest, None),
            P(rest, None),
            P(rest, None),
            P(rest, None),
        ),
        out_specs=(tokens, P()),
        check_vma=False,
    )
```

```python
import functools

import jax
import jax.numpy as jnp
from jax import lax
from jax.experimental import pallas as pl
from jax.experimental.pallas import tpu as pltpu
from jax.sharding import Mesh, PartitionSpec as P

IMG_TOK = 1024
AXES = ("x", "ylo", "z", "core", "yhi")
PLANE = ("ylo", "z", "yhi")
HALF = 640
DINO_Q = 384
SAM_Q = 64
SAM = 256
FEAT_Q = 512
COLS = HALF + DINO_Q
F32 = jnp.float32
BF16 = jnp.bfloat16
VMEM_LIMIT = 56 * 1024 * 1024


def ring(n, shift):
    return [(i, (i + shift) % n) for i in range(n)]


def dot(a, b):
    return jnp.dot(a, b, preferred_element_type=F32)


def dot_t(a, b):
    return lax.dot_general(a, b, (((1,), (1,)), ((), ())), preferred_element_type=F32)


def pick_cols(half):
    source = lax.broadcasted_iota(jnp.int32, (2 * HALF, HALF), 0)
    at = lax.broadcasted_iota(jnp.int32, (2 * HALF, HALF), 1)
    return (source == (at // 40) * 80 + half * 40 + at % 40).astype(BF16)


def gelu_slope(v):
    c = 0.7978845608028654
    t = jnp.tanh(c * (v + 0.044715 * (v * v * v)))
    return 0.5 * (1.0 + t) + 0.5 * v * (1.0 - t * t) * (c * (1.0 + 3.0 * 0.044715 * (v * v)))


def copies(refs, lo, hi, buf, sems, first=0):
    return [
        pltpu.make_async_copy(ref.at[:, pl.ds(lo, hi - lo)], buf.at[i], sems.at[first + i])
        for i, ref in enumerate(refs)
    ]


def target_kernel(f0, f1, f2, f3, gain_s, gain_d, goal_s, goal_d):
    parts = [f[...].astype(F32) for f in (f0, f1, f2, f3)]

    def center_of(lo, hi):
        cut = [p[:, lo:hi] for p in parts]
        chans = 4 * (hi - lo)
        center = sum(jnp.sum(p, axis=1, keepdims=True) for p in cut) / chans
        square = sum(jnp.sum(p * p, axis=1, keepdims=True) for p in cut) / chans
        return cut, center, lax.rsqrt(square - center * center + 1e-06)

    cut, center, root = center_of(0, DINO_Q)
    for j, part in enumerate(cut):
        goal_d[j] = ((part - center) * root * gain_d[j]).astype(BF16)
    cut, center, root = center_of(DINO_Q, DINO_Q + SAM_Q)
    for j, part in enumerate(cut):
        at = slice(j * SAM_Q, (j + 1) * SAM_Q)
        goal_s[:, at] = ((part - center) * root * gain_s[:, at]).astype(BF16)


def forward_kernel(
    where, tok_m, tok_o, pre0, goal_s, goal_d, live,
    m0, o0, m1, o1, m2, o2, m3, o3,
    pred_s, pred_d, pre, score, part, act, w_in, w_out, w_sam, sems,
):
    x, core = where[0], where[1]
    got_in = copies((m1, o1, m3, o3, m2, o2), 0, HALF, w_in, sems)
    got_out = copies((m0, o0, m1, o1, m3, o3, m2, o2), HALF, COLS, w_out, sems, 6)
    got_sam = copies((m2, o2), COLS, COLS + SAM, w_sam, sems, 14)
    for copy in got_in + got_out + got_sam:
        copy.start()
    for i, j in enumerate((0, 1, 3, 2)):
        if i == 0:
            value = pre0[...]
        else:
            got_in[2 * i - 2].wait()
            got_in[2 * i - 1].wait()
            value = dot(tok_m[...], w_in[2 * i - 2]) + dot(tok_o[...], w_in[2 * i - 1])
        at = lax.rem(x + j, 4)
        pre[at] = value
        act[at] = jax.nn.gelu(value).astype(BF16)

    def sums(value, aim):
        return [jnp.sum(v, axis=1, keepdims=True) for v in (value * value, aim * aim, value * aim)]

    found = [0.0, 0.0, 0.0]
    dm, do = act[2 + core], act[3 - core]
    for i, j in enumerate((0, 1, 3, 2)):
        got_out[2 * i].wait()
        got_out[2 * i + 1].wait()
        value = dot(dm, w_out[2 * i]) + dot(do, w_out[2 * i + 1])
        pred_d[j] = value
        found = [a + b for a, b in zip(found, sums(value, goal_d[j].astype(F32)))]
    for copy in got_sam:
        copy.wait()
    value = dot(act[core], w_sam[0]) + dot(act[1 - core], w_sam[1])
    pred_s[...] = value
    total = 0.0
    heads = ((SAM, sums(value, goal_s[...].astype(F32))), (4 * DINO_Q, found))
    for head, (chans, (pp, tt, pt)) in enumerate(heads):
        mean = pp / chans + 1e-05
        inv_root = lax.rsqrt(mean * (tt / chans + 1e-05))
        cosine = pt / chans * inv_root
        score[:, 2 * head:2 * head + 1] = inv_root
        score[:, 2 * head + 1:2 * head + 2] = cosine / mean
        total += cosine
    loss = jnp.sum(live[...] * (2.0 - total), axis=0, keepdims=True)
    part[...] = loss[:, :, None] + jnp.zeros(part.shape, F32)


def hidden_kernel(
    where, pred_s, pred_d, goal_s, goal_d, score, scale, pre,
    m0, o0, m1, o1, m2, o2, m3, o3,
    hid, w_out, w_sam, sems,
):
    core = where[1]
    got_sam = copies((m2, o2), COLS, COLS + SAM, w_sam, sems)
    got_out = copies((m0, o0, m1, o1, m2, o2, m3, o3), HALF, COLS, w_out, sems, 2)
    for copy in got_sam + got_out:
        copy.start()

    def back(head, pred, goal, chans):
        inv_root = score[:, 2 * head:2 * head + 1]
        ratio = score[:, 2 * head + 1:2 * head + 2]
        return (-scale[...] * (goal.astype(F32) * inv_root - ratio * pred) / chans).astype(BF16)

    def finish(head, found):
        for side, value in enumerate(found):
            at = 2 * head + (core if side == 0 else 1 - core)
            hid[at] = (value * gelu_slope(pre[at])).astype(BF16)

    value = back(0, pred_s[...], goal_s[...], SAM)
    for copy in got_sam:
        copy.wait()
    finish(0, [dot_t(value, w_sam[side]) for side in range(2)])
    found = [0.0, 0.0]
    for j in range(4):
        value = back(1, pred_d[j], goal_d[j], 4 * DINO_Q)
        for side in range(2):
            got_out[2 * j + side].wait()
            found[side] += dot_t(value, w_out[2 * j + side])
    finish(1, found)


def grad_kernel(where, hid, m0, o0, m1, o1, m2, o2, m3, o3, grad, w_in, sems):
    x, core = where[0], where[1]
    got = copies((m0, o0, m1, o1, m2, o2, m3, o3), 0, HALF, w_in, sems)
    for copy in got:
        copy.start()
    total = [0.0, 0.0]
    for j in range(4):
        h = hid[lax.rem(x + j, 4)]
        for side in range(2):
            got[2 * j + side].wait()
            total[side] += dot_t(h, w_in[2 * j + side])
    at = lax.broadcasted_iota(jnp.int32, (1, HALF), 1)
    block = (at * 1639) >> 16
    row = lax.broadcasted_iota(jnp.int32, (2 * HALF, HALF), 0)
    whole = 0.0
    for side, half in enumerate((core, 1 - core)):
        source = at + block * 40 + half * 40
        whole += dot_t(total[side].astype(BF16), (row == source).astype(BF16))
    grad[...] = whole.astype(BF16)


def shards(
    student_tokens,
    sam_maps,
    dino_maps,
    sam_gain,
    dino_gain,
    patch_counts,
    sam_in,
    sam_out,
    dino_in,
    dino_out,
):
    rows = student_tokens.shape[0]
    x = lax.axis_index("x")
    core = lax.axis_index("core")
    shard = sam_in.shape[0]

    both = jnp.concatenate([sam_in, dino_in], axis=0)
    picked = dot(both, pick_cols(x % 2)).astype(BF16).reshape(2, shard, HALF)

    def payload(q, extra):
        part_in = lax.dynamic_index_in_dim(picked, q // 2, axis=0, keepdims=False)
        part_d = lax.dynamic_slice(dino_out, (0, q * DINO_Q), (shard, DINO_Q))
        part = jnp.concatenate([part_in, part_d] + extra, axis=1)
        cols = part.shape[1]
        return jnp.broadcast_to(part.reshape(1, shard // 2, 2, cols), (64, shard // 2, 2, cols))

    def gather_plane(many):
        return lax.all_to_all(many, PLANE, split_axis=0, concat_axis=0, tiled=True)

    own_b = payload(x, [])
    sam4 = sam_out.reshape(shard, 4, SAM_Q)
    sam_parts = [lax.dynamic_index_in_dim(sam4, (x + j) % 4, axis=1, keepdims=False) for j in range(4)]
    opp_b, dino_maps, sam_maps = lax.optimization_barrier(
        (payload((x + 2) % 4, sam_parts), dino_maps, sam_maps))
    feats = jnp.concatenate(
        [dino_maps, sam_maps, jnp.zeros((4, rows, FEAT_Q - DINO_Q - SAM_Q), BF16)], axis=2)

    def feat_for(slot):
        return lax.dynamic_index_in_dim(feats, (x - slot) % 4, axis=0, keepdims=False)

    got = [feat_for(0)] + [lax.ppermute(feat_for(s), "x", ring(4, -s)) for s in (1, 2, 3)]
    tok_m = dot(student_tokens, pick_cols(core)).astype(BF16)
    tok_o = dot(student_tokens, pick_cols(1 - core)).astype(BF16)

    own_g = gather_plane(own_b)
    start = lax.axis_index(AXES) * rows
    limit = lax.dynamic_index_in_dim(patch_counts, start // IMG_TOK, keepdims=False)
    slot_at = start % IMG_TOK + jnp.arange(rows, dtype=jnp.int32)
    live = (slot_at < limit).astype(F32)[:, None]
    count = jnp.sum(jnp.clip(patch_counts, 0, IMG_TOK)).astype(F32)

    place = jnp.stack([x, core]).astype(jnp.int32)
    scale = live / count
    def gains(gain, width):
        return [lax.dynamic_slice(gain, ((x + j) % 4 * width,), (width,)) for j in range(4)]

    in_vmem = pl.BlockSpec(memory_space=pltpu.VMEM)
    goal_s, goal_d = pl.pallas_call(
        target_kernel,
        out_shape=(
            jax.ShapeDtypeStruct((rows, SAM), BF16),
            jax.ShapeDtypeStruct((4, rows, DINO_Q), BF16),
        ),
        in_specs=[in_vmem] * 6,
        out_specs=(in_vmem,) * 2,
        name="target",
    )(*got, jnp.concatenate(gains(sam_gain, SAM_Q))[None, :], jnp.stack(gains(dino_gain, DINO_Q))[:, None, :])
    own, opp_b, goal_s, goal_d, tok_m, tok_o, live, scale, place = lax.optimization_barrier(
        (own_g.reshape(HALF, COLS), opp_b, goal_s, goal_d, tok_m, tok_o, live, scale, place))
    opp_g = gather_plane(opp_b)

    def swap(value):
        return lax.ppermute(value, "core", ring(2, 1))


    next_m = lax.ppermute(own, "x", ring(4, -1))
    prev_m = lax.ppermute(own, "x", ring(4, 1))
    own_o = swap(own)
    pre0 = dot(tok_m, own[:, :HALF]) + dot(tok_o, own_o[:, :HALF])
    next_m, prev_m = lax.optimization_barrier((next_m, prev_m))
    next_o, prev_o = swap(next_m), swap(prev_m)
    opp_g, pre0 = lax.optimization_barrier((opp_g, pre0))
    opp = opp_g.reshape(HALF, COLS + SAM)
    opp, next_o, prev_o = lax.optimization_barrier((opp, next_o, prev_o))
    slots = [(own, own_o), (next_m, next_o), (opp, swap(opp)), (prev_m, prev_o)]
    flat = [w for pair in slots for w in pair]
    anywhere = pl.BlockSpec(memory_space=pl.ANY)
    in_smem = pl.BlockSpec(memory_space=pltpu.SMEM)
    params = pltpu.CompilerParams(vmem_limit_bytes=VMEM_LIMIT)
    pred_s, pred_d, pre, score, loss = pl.pallas_call(
        forward_kernel,
        out_shape=(
            jax.ShapeDtypeStruct((rows, SAM), F32),
            jax.ShapeDtypeStruct((4, rows, DINO_Q), F32),
            jax.ShapeDtypeStruct((4, rows, HALF), F32),
            jax.ShapeDtypeStruct((rows, 4), F32),
            jax.ShapeDtypeStruct((16, 1, 128), F32),
        ),
        in_specs=[in_smem] + [in_vmem] * 6 + [anywhere] * 8,
        out_specs=(in_vmem,) * 5,
        scratch_shapes=[
            pltpu.VMEM((4, rows, HALF), BF16),
            pltpu.VMEM((6, HALF, HALF), BF16),
            pltpu.VMEM((8, HALF, DINO_Q), BF16),
            pltpu.VMEM((2, HALF, SAM), BF16),
            pltpu.SemaphoreType.DMA((16,)),
        ],
        compiler_params=params,
        name="forward",
    )(place, tok_m, tok_o, pre0, goal_s, goal_d, live, *flat)

    loss = lax.all_to_all(loss, ("z", "core"), split_axis=0, concat_axis=0, tiled=True)
    hid = pl.pallas_call(
        hidden_kernel,
        out_shape=jax.ShapeDtypeStruct((4, rows, HALF), BF16),
        in_specs=[in_smem] + [in_vmem] * 7 + [anywhere] * 8,
        out_specs=in_vmem,
        scratch_shapes=[
            pltpu.VMEM((8, HALF, DINO_Q), BF16),
            pltpu.VMEM((2, HALF, SAM), BF16),
            pltpu.SemaphoreType.DMA((10,)),
        ],
        compiler_params=params,
        name="hidden",
    )(place, pred_s, pred_d, goal_s, goal_d, score, scale, pre, *flat)

    loss = jnp.broadcast_to(jnp.sum(loss, axis=0, keepdims=True), (32, 1, 128))
    loss, hid = lax.optimization_barrier((loss, hid))
    loss = lax.all_to_all(loss, ("x", "ylo", "yhi"), split_axis=0, concat_axis=0, tiled=True)
    loss = jnp.sum(loss[:, 0, 0]) / count

    grad = pl.pallas_call(
        grad_kernel,
        out_shape=jax.ShapeDtypeStruct((rows, 2 * HALF), BF16),
        in_specs=[in_smem, in_vmem] + [anywhere] * 8,
        out_specs=in_vmem,
        scratch_shapes=[pltpu.VMEM((8, HALF, HALF), BF16), pltpu.SemaphoreType.DMA((8,))],
        compiler_params=params,
        name="grad",
    )(place, hid, *flat)
    return (grad, loss)


def solution(mesh):
    fine = Mesh(mesh.devices.reshape(4, 2, 8, 2, 4), AXES)
    tokens = P(AXES, None)
    rest = ("ylo", "z", "core", "yhi")
    return jax.shard_map(
        shards,
        mesh=fine,
        in_specs=(
            tokens,
            P(None, rest, "x"),
            P(None, rest, "x"),
            P(),
            P(),
            P(),
            P(rest, None),
            P(rest, None),
            P(rest, None),
            P(rest, None),
        ),
        out_specs=(tokens, P()),
        check_vma=False,
    )
```

```python
import functools

import jax
import jax.numpy as jnp
from jax import lax
from jax.experimental import pallas as pl
from jax.experimental.pallas import tpu as pltpu
from jax.sharding import Mesh, PartitionSpec as P

IMG_TOK = 1024
AXES = ("x", "ylo", "z", "core", "yhi")
PLANE = ("ylo", "z", "yhi")
HALF = 640
DINO_Q = 384
SAM_Q = 64
SAM = 256
FEAT_Q = 512
COLS = HALF + DINO_Q
DINO = 4 * DINO_Q
F32 = jnp.float32
BF16 = jnp.bfloat16
VMEM_LIMIT = 56 * 1024 * 1024


def ring(n, shift):
    return [(i, (i + shift) % n) for i in range(n)]


def dot(a, b):
    return jnp.dot(a, b, preferred_element_type=F32)


def dot_t(a, b):
    return lax.dot_general(a, b, (((1,), (1,)), ((), ())), preferred_element_type=F32)


def pick_cols(half):
    source = lax.broadcasted_iota(jnp.int32, (2 * HALF, HALF), 0)
    at = lax.broadcasted_iota(jnp.int32, (2 * HALF, HALF), 1)
    return (source == (at // 40) * 80 + half * 40 + at % 40).astype(BF16)


def gelu_slope(v):
    c = 0.7978845608028654
    t = jnp.tanh(c * (v + 0.044715 * (v * v * v)))
    return 0.5 * (1.0 + t) + 0.5 * v * (1.0 - t * t) * (c * (1.0 + 3.0 * 0.044715 * (v * v)))


def copies(refs, lo, hi, buf, sems, first=0):
    return [
        pltpu.make_async_copy(ref.at[:, pl.ds(lo, hi - lo)], buf.at[i], sems.at[first + i])
        for i, ref in enumerate(refs)
    ]


def side_by_side(mine, other, lo, hi, buf, sems, first=0):
    width = hi - lo
    return [
        pltpu.make_async_copy(
            ref.at[:, pl.ds(lo, width)],
            buf.at[side, :, pl.ds(j * width, width)],
            sems.at[first + 4 * side + j],
        )
        for side, refs in enumerate((mine, other))
        for j, ref in enumerate(refs)
    ]


def dots(product, left, got, right):
    out = []
    for side in range(2):
        for copy in got[4 * side:4 * side + 4]:
            copy.wait()
        out.append(product(left[side], right[side]))
    return out


def target_kernel(f0, f1, f2, f3, gain_s, gain_d, goal_s, goal_d):
    parts = [f[...].astype(F32) for f in (f0, f1, f2, f3)]

    def center_of(lo, hi):
        cut = [p[:, lo:hi] for p in parts]
        chans = 4 * (hi - lo)
        center = sum(jnp.sum(p, axis=1, keepdims=True) for p in cut) / chans
        square = sum(jnp.sum(p * p, axis=1, keepdims=True) for p in cut) / chans
        return cut, center, lax.rsqrt(square - center * center + 1e-06)

    cut, center, root = center_of(0, DINO_Q)
    for j, part in enumerate(cut):
        at = slice(j * DINO_Q, (j + 1) * DINO_Q)
        goal_d[:, at] = ((part - center) * root * gain_d[:, at]).astype(BF16)
    cut, center, root = center_of(DINO_Q, DINO_Q + SAM_Q)
    for j, part in enumerate(cut):
        at = slice(j * SAM_Q, (j + 1) * SAM_Q)
        goal_s[:, at] = ((part - center) * root * gain_s[:, at]).astype(BF16)


def forward_kernel(
    where, tok_m, tok_o, pre0, goal_s, goal_d, live,
    m0, o0, m1, o1, m2, o2, m3, o3,
    pred_s, pred_d, pre, score, part, act, w_in, w_out, w_sam, sems,
):
    x, core = where[0], where[1]
    got_in = copies((m1, o1, m3, o3, m2, o2), 0, HALF, w_in, sems)
    got_out = side_by_side((m0, m1, m2, m3), (o0, o1, o2, o3), HALF, COLS, w_out, sems, 6)
    got_sam = copies((m2, o2), COLS, COLS + SAM, w_sam, sems, 14)
    for copy in got_in + got_out + got_sam:
        copy.start()
    for i, j in enumerate((0, 1, 3, 2)):
        if i == 0:
            value = pre0[...]
        else:
            got_in[2 * i - 2].wait()
            got_in[2 * i - 1].wait()
            value = dot(tok_m[...], w_in[2 * i - 2]) + dot(tok_o[...], w_in[2 * i - 1])
        at = lax.rem(x + j, 4)
        pre[at] = value
        act[at] = jax.nn.gelu(value).astype(BF16)

    def sums(value, aim):
        return [jnp.sum(v, axis=1, keepdims=True) for v in (value * value, aim * aim, value * aim)]

    value = sum(dots(dot, (act[2 + core], act[3 - core]), got_out, w_out))
    pred_d[...] = value
    found = sums(value, goal_d[...].astype(F32))
    for copy in got_sam:
        copy.wait()
    value = dot(act[core], w_sam[0]) + dot(act[1 - core], w_sam[1])
    pred_s[...] = value
    total = 0.0
    heads = ((SAM, sums(value, goal_s[...].astype(F32))), (DINO, found))
    for head, (chans, (pp, tt, pt)) in enumerate(heads):
        mean = pp / chans + 1e-05
        inv_root = lax.rsqrt(mean * (tt / chans + 1e-05))
        cosine = pt / chans * inv_root
        score[:, 2 * head:2 * head + 1] = inv_root
        score[:, 2 * head + 1:2 * head + 2] = cosine / mean
        total += cosine
    loss = jnp.sum(live[...] * (2.0 - total), axis=0, keepdims=True)
    part[...] = loss[:, :, None] + jnp.zeros(part.shape, F32)


def hidden_kernel(
    where, pred_s, pred_d, goal_s, goal_d, score, scale, pre,
    m0, o0, m1, o1, m2, o2, m3, o3,
    hid, w_out, w_sam, sems,
):
    core = where[1]
    got_sam = copies((m2, o2), COLS, COLS + SAM, w_sam, sems)
    got_out = side_by_side((m0, m1, m2, m3), (o0, o1, o2, o3), HALF, COLS, w_out, sems, 2)
    for copy in got_sam + got_out:
        copy.start()

    def back(head, pred, goal, chans):
        inv_root = score[:, 2 * head:2 * head + 1]
        ratio = score[:, 2 * head + 1:2 * head + 2]
        return (-scale[...] * (goal.astype(F32) * inv_root - ratio * pred) / chans).astype(BF16)

    def finish(head, found):
        for side, value in enumerate(found):
            at = 2 * head + (core if side == 0 else 1 - core)
            hid[at] = (value * gelu_slope(pre[at])).astype(BF16)

    value = back(0, pred_s[...], goal_s[...], SAM)
    for copy in got_sam:
        copy.wait()
    finish(0, [dot_t(value, w_sam[side]) for side in range(2)])
    value = back(1, pred_d[...], goal_d[...], DINO)
    finish(1, dots(dot_t, (value, value), got_out, w_out))


def grad_kernel(where, hid, m0, o0, m1, o1, m2, o2, m3, o3, grad, slots, w_in, sems):
    x, core = where[0], where[1]
    got = side_by_side((m0, m1, m2, m3), (o0, o1, o2, o3), 0, HALF, w_in, sems)
    for copy in got:
        copy.start()
    for j in range(4):
        slots[:, j * HALF:(j + 1) * HALF] = hid[lax.rem(x + j, 4)]
    total = dots(dot_t, (slots[...], slots[...]), got, w_in)
    at = lax.broadcasted_iota(jnp.int32, (1, HALF), 1)
    block = (at * 1639) >> 16
    row = lax.broadcasted_iota(jnp.int32, (2 * HALF, HALF), 0)
    whole = 0.0
    for side, half in enumerate((core, 1 - core)):
        source = at + block * 40 + half * 40
        whole += dot_t(total[side].astype(BF16), (row == source).astype(BF16))
    grad[...] = whole.astype(BF16)


def rows_kernel(pairs, rows):
    rows[...] = pairs[...].reshape(rows.shape)


def full_rows(got):
    pairs = got.reshape(HALF // 2, 2, got.shape[3])
    cols = got.shape[3]
    return pl.pallas_call(
        rows_kernel,
        out_shape=jax.ShapeDtypeStruct((HALF, cols), BF16),
        grid=(2,),
        in_specs=[pl.BlockSpec((HALF // 4, 2, cols), lambda i: (i, 0, 0))],
        out_specs=pl.BlockSpec((HALF // 2, cols), lambda i: (i, 0)),
        compiler_params=pltpu.CompilerParams(vmem_limit_bytes=VMEM_LIMIT),
        name="rows",
    )(pairs)


def shards(
    student_tokens,
    sam_maps,
    dino_maps,
    sam_gain,
    dino_gain,
    patch_counts,
    sam_in,
    sam_out,
    dino_in,
    dino_out,
):
    rows = student_tokens.shape[0]
    x = lax.axis_index("x")
    core = lax.axis_index("core")
    shard = sam_in.shape[0]

    both = jnp.concatenate([sam_in, dino_in], axis=0)
    picked = dot(both, pick_cols(x % 2)).astype(BF16).reshape(2, shard, HALF)

    def payload(q, extra):
        part_in = lax.dynamic_index_in_dim(picked, q // 2, axis=0, keepdims=False)
        part_d = lax.dynamic_slice(dino_out, (0, q * DINO_Q), (shard, DINO_Q))
        part = jnp.concatenate([part_in, part_d] + extra, axis=1)
        cols = part.shape[1]
        return jnp.broadcast_to(part.reshape(1, shard // 2, 2, cols), (64, shard // 2, 2, cols))

    def gather_plane(many):
        return lax.all_to_all(many, PLANE, split_axis=0, concat_axis=0, tiled=True)

    own_b = payload(x, [])
    sam4 = sam_out.reshape(shard, 4, SAM_Q)
    sam_parts = [lax.dynamic_index_in_dim(sam4, (x + j) % 4, axis=1, keepdims=False) for j in range(4)]
    opp_b, dino_maps, sam_maps = lax.optimization_barrier(
        (payload((x + 2) % 4, sam_parts), dino_maps, sam_maps))
    feats = jnp.concatenate(
        [dino_maps, sam_maps, jnp.zeros((4, rows, FEAT_Q - DINO_Q - SAM_Q), BF16)], axis=2)

    def feat_for(slot):
        return lax.dynamic_index_in_dim(feats, (x - slot) % 4, axis=0, keepdims=False)

    got = [feat_for(0)] + [lax.ppermute(feat_for(s), "x", ring(4, -s)) for s in (1, 2, 3)]
    tok_m = dot(student_tokens, pick_cols(core)).astype(BF16)
    tok_o = dot(student_tokens, pick_cols(1 - core)).astype(BF16)

    own_g = gather_plane(own_b)
    start = lax.axis_index(AXES) * rows
    limit = lax.dynamic_index_in_dim(patch_counts, start // IMG_TOK, keepdims=False)
    slot_at = start % IMG_TOK + jnp.arange(rows, dtype=jnp.int32)
    live = (slot_at < limit).astype(F32)[:, None]
    count = jnp.sum(jnp.clip(patch_counts, 0, IMG_TOK)).astype(F32)

    place = jnp.stack([x, core]).astype(jnp.int32)
    scale = live / count
    def gains(gain, width):
        return [lax.dynamic_slice(gain, ((x + j) % 4 * width,), (width,)) for j in range(4)]

    in_vmem = pl.BlockSpec(memory_space=pltpu.VMEM)
    goal_s, goal_d = pl.pallas_call(
        target_kernel,
        out_shape=(
            jax.ShapeDtypeStruct((rows, SAM), BF16),
            jax.ShapeDtypeStruct((rows, DINO), BF16),
        ),
        in_specs=[in_vmem] * 6,
        out_specs=(in_vmem,) * 2,
        name="target",
    )(*got, jnp.concatenate(gains(sam_gain, SAM_Q))[None, :], jnp.concatenate(gains(dino_gain, DINO_Q))[None, :])
    own, opp_b, goal_s, goal_d, tok_m, tok_o, live, scale, place = lax.optimization_barrier(
        (own_g.reshape(HALF, COLS), opp_b, goal_s, goal_d, tok_m, tok_o, live, scale, place))
    opp_g = gather_plane(opp_b)

    def swap(value):
        return lax.ppermute(value, "core", ring(2, 1))


    next_m = lax.ppermute(own, "x", ring(4, -1))
    prev_m = lax.ppermute(own, "x", ring(4, 1))
    own_o = swap(own)
    pre0 = dot(tok_m, own[:, :HALF]) + dot(tok_o, own_o[:, :HALF])
    next_m, prev_m = lax.optimization_barrier((next_m, prev_m))
    next_o, prev_o = swap(next_m), swap(prev_m)
    opp_g, pre0 = lax.optimization_barrier((opp_g, pre0))
    opp = full_rows(opp_g)
    opp, next_o, prev_o = lax.optimization_barrier((opp, next_o, prev_o))
    slots = [(own, own_o), (next_m, next_o), (opp, swap(opp)), (prev_m, prev_o)]
    flat = [w for pair in slots for w in pair]
    anywhere = pl.BlockSpec(memory_space=pl.ANY)
    in_smem = pl.BlockSpec(memory_space=pltpu.SMEM)
    params = pltpu.CompilerParams(vmem_limit_bytes=VMEM_LIMIT)
    pred_s, pred_d, pre, score, loss = pl.pallas_call(
        forward_kernel,
        out_shape=(
            jax.ShapeDtypeStruct((rows, SAM), F32),
            jax.ShapeDtypeStruct((rows, DINO), F32),
            jax.ShapeDtypeStruct((4, rows, HALF), F32),
            jax.ShapeDtypeStruct((rows, 4), F32),
            jax.ShapeDtypeStruct((16, 1, 128), F32),
        ),
        in_specs=[in_smem] + [in_vmem] * 6 + [anywhere] * 8,
        out_specs=(in_vmem,) * 5,
        scratch_shapes=[
            pltpu.VMEM((4, rows, HALF), BF16),
            pltpu.VMEM((6, HALF, HALF), BF16),
            pltpu.VMEM((2, HALF, DINO), BF16),
            pltpu.VMEM((2, HALF, SAM), BF16),
            pltpu.SemaphoreType.DMA((16,)),
        ],
        compiler_params=params,
        name="forward",
    )(place, tok_m, tok_o, pre0, goal_s, goal_d, live, *flat)

    loss = lax.all_to_all(loss, ("z", "core"), split_axis=0, concat_axis=0, tiled=True)
    hid = pl.pallas_call(
        hidden_kernel,
        out_shape=jax.ShapeDtypeStruct((4, rows, HALF), BF16),
        in_specs=[in_smem] + [in_vmem] * 7 + [anywhere] * 8,
        out_specs=in_vmem,
        scratch_shapes=[
            pltpu.VMEM((2, HALF, DINO), BF16),
            pltpu.VMEM((2, HALF, SAM), BF16),
            pltpu.SemaphoreType.DMA((10,)),
        ],
        compiler_params=params,
        name="hidden",
    )(place, pred_s, pred_d, goal_s, goal_d, score, scale, pre, *flat)

    loss = jnp.broadcast_to(jnp.sum(loss, axis=0, keepdims=True), (32, 1, 128))
    loss, hid = lax.optimization_barrier((loss, hid))
    loss = lax.all_to_all(loss, ("x", "ylo", "yhi"), split_axis=0, concat_axis=0, tiled=True)
    loss = jnp.sum(loss[:, 0, 0]) / count

    grad = pl.pallas_call(
        grad_kernel,
        out_shape=jax.ShapeDtypeStruct((rows, 2 * HALF), BF16),
        in_specs=[in_smem, in_vmem] + [anywhere] * 8,
        out_specs=in_vmem,
        scratch_shapes=[
            pltpu.VMEM((rows, 4 * HALF), BF16),
            pltpu.VMEM((2, HALF, 4 * HALF), BF16),
            pltpu.SemaphoreType.DMA((8,)),
        ],
        compiler_params=params,
        name="grad",
    )(place, hid, *flat)
    return (grad, loss)


def solution(mesh):
    fine = Mesh(mesh.devices.reshape(4, 2, 8, 2, 4), AXES)
    tokens = P(AXES, None)
    rest = ("ylo", "z", "core", "yhi")
    return jax.shard_map(
        shards,
        mesh=fine,
        in_specs=(
            tokens,
            P(None, rest, "x"),
            P(None, rest, "x"),
            P(),
            P(),
            P(),
            P(rest, None),
            P(rest, None),
            P(rest, None),
            P(rest, None),
        ),
        out_specs=(tokens, P()),
        check_vma=False,
    )
```

```python
import functools

import jax
import jax.numpy as jnp
from jax import lax
from jax.experimental import pallas as pl
from jax.experimental.pallas import tpu as pltpu
from jax.sharding import Mesh, PartitionSpec as P

IMG_TOK = 1024
AXES = ("x", "ylo", "z", "core", "yhi")
PLANE = ("ylo", "z", "yhi")
HALF = 640
DINO_Q = 384
SAM_Q = 64
SAM = 256
FEAT_Q = 512
COLS = HALF + DINO_Q
DINO = 4 * DINO_Q
F32 = jnp.float32
BF16 = jnp.bfloat16
VMEM_LIMIT = 56 * 1024 * 1024


def ring(n, shift):
    return [(i, (i + shift) % n) for i in range(n)]


def dot(a, b):
    return jnp.dot(a, b, preferred_element_type=F32)


def dot_t(a, b):
    return lax.dot_general(a, b, (((1,), (1,)), ((), ())), preferred_element_type=F32)


def pick_cols(half):
    source = lax.broadcasted_iota(jnp.int32, (2 * HALF, HALF), 0)
    at = lax.broadcasted_iota(jnp.int32, (2 * HALF, HALF), 1)
    return (source == (at // 40) * 80 + half * 40 + at % 40).astype(BF16)


def gelu_slope(v):
    c = 0.7978845608028654
    t = jnp.tanh(c * (v + 0.044715 * (v * v * v)))
    return 0.5 * (1.0 + t) + 0.5 * v * (1.0 - t * t) * (c * (1.0 + 3.0 * 0.044715 * (v * v)))


def copies(refs, lo, hi, buf, sems, first=0):
    return [
        pltpu.make_async_copy(ref.at[:, pl.ds(lo, hi - lo)], buf.at[i], sems.at[first + i])
        for i, ref in enumerate(refs)
    ]


def side_by_side(mine, other, lo, hi, buf, sems, first=0):
    width = hi - lo
    return [
        pltpu.make_async_copy(
            ref.at[:, pl.ds(lo, width)],
            buf.at[side, :, pl.ds(j * width, width)],
            sems.at[first + 4 * side + j],
        )
        for side, refs in enumerate((mine, other))
        for j, ref in enumerate(refs)
    ]


def dots(product, left, got, right):
    out = []
    for side in range(2):
        for copy in got[4 * side:4 * side + 4]:
            copy.wait()
        out.append(product(left[side], right[side]))
    return out


def target_kernel(f0, f1, f2, f3, gain_s, gain_d, goal_s, goal_d):
    parts = [f[...].astype(F32) for f in (f0, f1, f2, f3)]

    def center_of(lo, hi):
        cut = [p[:, lo:hi] for p in parts]
        chans = 4 * (hi - lo)
        center = sum(jnp.sum(p, axis=1, keepdims=True) for p in cut) / chans
        square = sum(jnp.sum(p * p, axis=1, keepdims=True) for p in cut) / chans
        return cut, center, lax.rsqrt(square - center * center + 1e-06)

    cut, center, root = center_of(0, DINO_Q)
    for j, part in enumerate(cut):
        at = slice(j * DINO_Q, (j + 1) * DINO_Q)
        goal_d[:, at] = ((part - center) * root * gain_d[:, at]).astype(BF16)
    cut, center, root = center_of(DINO_Q, DINO_Q + SAM_Q)
    for j, part in enumerate(cut):
        at = slice(j * SAM_Q, (j + 1) * SAM_Q)
        goal_s[:, at] = ((part - center) * root * gain_s[:, at]).astype(BF16)


def forward_kernel(
    where, tok_m, tok_o, pre0, goal_s, goal_d, live,
    m0, o0, m1, o1, m2, o2, m3, o3,
    pred_s, pred_d, pre, score, part, act, w_in, w_out, w_sam, sems,
):
    x, core = where[0], where[1]
    got_in = copies((m1, o1, m3, o3, m2, o2), 0, HALF, w_in, sems)
    got_out = side_by_side((m0, m1, m2, m3), (o0, o1, o2, o3), HALF, COLS, w_out, sems, 6)
    got_sam = copies((m2, o2), COLS, COLS + SAM, w_sam, sems, 14)
    for copy in got_in + got_out + got_sam:
        copy.start()
    for i, j in enumerate((0, 1, 3, 2)):
        if i == 0:
            value = pre0[...]
        else:
            got_in[2 * i - 2].wait()
            got_in[2 * i - 1].wait()
            value = dot(tok_m[...], w_in[2 * i - 2]) + dot(tok_o[...], w_in[2 * i - 1])
        at = lax.rem(x + j, 4)
        pre[at] = value
        act[at] = jax.nn.gelu(value).astype(BF16)

    def sums(value, aim):
        return [jnp.sum(v, axis=1, keepdims=True) for v in (value * value, aim * aim, value * aim)]

    value = sum(dots(dot, (act[2 + core], act[3 - core]), got_out, w_out))
    pred_d[...] = value
    found = sums(value, goal_d[...].astype(F32))
    for copy in got_sam:
        copy.wait()
    value = dot(act[core], w_sam[0]) + dot(act[1 - core], w_sam[1])
    pred_s[...] = value
    total = 0.0
    heads = ((SAM, sums(value, goal_s[...].astype(F32))), (DINO, found))
    for head, (chans, (pp, tt, pt)) in enumerate(heads):
        mean = pp / chans + 1e-05
        inv_root = lax.rsqrt(mean * (tt / chans + 1e-05))
        cosine = pt / chans * inv_root
        score[:, 2 * head:2 * head + 1] = inv_root
        score[:, 2 * head + 1:2 * head + 2] = cosine / mean
        total += cosine
    loss = jnp.sum(live[...] * (2.0 - total), axis=0, keepdims=True)
    part[...] = loss[:, :, None] + jnp.zeros(part.shape, F32)


def hidden_kernel(
    where, pred_s, pred_d, goal_s, goal_d, score, scale, pre,
    m0, o0, m1, o1, m2, o2, m3, o3,
    hid, w_out, w_sam, sems,
):
    core = where[1]
    got_sam = copies((m2, o2), COLS, COLS + SAM, w_sam, sems)
    got_out = side_by_side((m0, m1, m2, m3), (o0, o1, o2, o3), HALF, COLS, w_out, sems, 2)
    for copy in got_sam + got_out:
        copy.start()

    def back(head, pred, goal, chans):
        inv_root = score[:, 2 * head:2 * head + 1]
        ratio = score[:, 2 * head + 1:2 * head + 2]
        return (-scale[...] * (goal.astype(F32) * inv_root - ratio * pred) / chans).astype(BF16)

    def finish(head, found):
        for side, value in enumerate(found):
            at = 2 * head + (core if side == 0 else 1 - core)
            hid[at] = (value * gelu_slope(pre[at])).astype(BF16)

    value = back(0, pred_s[...], goal_s[...], SAM)
    for copy in got_sam:
        copy.wait()
    finish(0, [dot_t(value, w_sam[side]) for side in range(2)])
    value = back(1, pred_d[...], goal_d[...], DINO)
    finish(1, dots(dot_t, (value, value), got_out, w_out))


def grad_kernel(where, hid, m0, o0, m1, o1, m2, o2, m3, o3, grad, slots, w_in, sems):
    x, core = where[0], where[1]
    got = side_by_side((m0, m1, m2, m3), (o0, o1, o2, o3), 0, HALF, w_in, sems)
    for copy in got:
        copy.start()
    for j in range(4):
        slots[:, j * HALF:(j + 1) * HALF] = hid[lax.rem(x + j, 4)]
    total = dots(dot_t, (slots[...], slots[...]), got, w_in)
    at = lax.broadcasted_iota(jnp.int32, (1, HALF), 1)
    block = (at * 1639) >> 16
    row = lax.broadcasted_iota(jnp.int32, (2 * HALF, HALF), 0)
    whole = 0.0
    for side, half in enumerate((core, 1 - core)):
        source = at + block * 40 + half * 40
        whole += dot_t(total[side].astype(BF16), (row == source).astype(BF16))
    grad[...] = whole.astype(BF16)


def rows_kernel(pairs, rows):
    rows[...] = pairs[...].reshape(rows.shape)


def full_rows(got):
    pairs = got.reshape(HALF // 2, 2, got.shape[3])
    cols = got.shape[3]
    return pl.pallas_call(
        rows_kernel,
        out_shape=jax.ShapeDtypeStruct((HALF, cols), BF16),
        grid=(2,),
        in_specs=[pl.BlockSpec((HALF // 4, 2, cols), lambda i: (i, 0, 0))],
        out_specs=pl.BlockSpec((HALF // 2, cols), lambda i: (i, 0)),
        compiler_params=pltpu.CompilerParams(vmem_limit_bytes=VMEM_LIMIT),
        name="rows",
    )(pairs)


def shards(
    student_tokens,
    sam_maps,
    dino_maps,
    sam_gain,
    dino_gain,
    patch_counts,
    sam_in,
    sam_out,
    dino_in,
    dino_out,
):
    rows = student_tokens.shape[0]
    x = lax.axis_index("x")
    core = lax.axis_index("core")
    shard = sam_in.shape[0]

    both = jnp.concatenate([sam_in, dino_in], axis=0)
    picked = dot(both, pick_cols(x % 2)).astype(BF16).reshape(2, shard, HALF)

    def payload(q, extra):
        part_in = lax.dynamic_index_in_dim(picked, q // 2, axis=0, keepdims=False)
        part_d = lax.dynamic_slice(dino_out, (0, q * DINO_Q), (shard, DINO_Q))
        part = jnp.concatenate([part_in, part_d] + extra, axis=1)
        cols = part.shape[1]
        return jnp.broadcast_to(part.reshape(1, shard // 2, 2, cols), (64, shard // 2, 2, cols))

    def gather_plane(many):
        return lax.all_to_all(many, PLANE, split_axis=0, concat_axis=0, tiled=True)

    own_b = payload(x, [])
    sam4 = sam_out.reshape(shard, 4, SAM_Q)
    sam_parts = [lax.dynamic_index_in_dim(sam4, (x + j) % 4, axis=1, keepdims=False) for j in range(4)]
    opp_b, dino_maps, sam_maps = lax.optimization_barrier(
        (payload((x + 2) % 4, sam_parts), dino_maps, sam_maps))
    feats = jnp.concatenate(
        [dino_maps, sam_maps, jnp.zeros((4, rows, FEAT_Q - DINO_Q - SAM_Q), BF16)], axis=2)

    def feat_for(slot):
        return lax.dynamic_index_in_dim(feats, (x - slot) % 4, axis=0, keepdims=False)

    got = [feat_for(0)] + [lax.ppermute(feat_for(s), "x", ring(4, -s)) for s in (1, 2, 3)]
    tok_m = dot(student_tokens, pick_cols(core)).astype(BF16)
    tok_o = dot(student_tokens, pick_cols(1 - core)).astype(BF16)

    own_g = gather_plane(own_b)
    start = lax.axis_index(AXES) * rows
    limit = lax.dynamic_index_in_dim(patch_counts, start // IMG_TOK, keepdims=False)
    slot_at = start % IMG_TOK + jnp.arange(rows, dtype=jnp.int32)
    live = (slot_at < limit).astype(F32)[:, None]
    count = jnp.sum(jnp.clip(patch_counts, 0, IMG_TOK)).astype(F32)

    place = jnp.stack([x, core]).astype(jnp.int32)
    scale = live / count
    def gains(gain, width):
        return [lax.dynamic_slice(gain, ((x + j) % 4 * width,), (width,)) for j in range(4)]

    in_vmem = pl.BlockSpec(memory_space=pltpu.VMEM)
    goal_s, goal_d = pl.pallas_call(
        target_kernel,
        out_shape=(
            jax.ShapeDtypeStruct((rows, SAM), BF16),
            jax.ShapeDtypeStruct((rows, DINO), BF16),
        ),
        in_specs=[in_vmem] * 6,
        out_specs=(in_vmem,) * 2,
        name="target",
    )(*got, jnp.concatenate(gains(sam_gain, SAM_Q))[None, :], jnp.concatenate(gains(dino_gain, DINO_Q))[None, :])
    own, opp_b, goal_s, goal_d, tok_m, tok_o, live, scale, place = lax.optimization_barrier(
        (own_g.reshape(HALF, COLS), opp_b, goal_s, goal_d, tok_m, tok_o, live, scale, place))
    opp_g = gather_plane(opp_b)

    def swap(value):
        return lax.ppermute(value, "core", ring(2, 1))


    next_m = lax.ppermute(own, "x", ring(4, -1))
    prev_m = lax.ppermute(own, "x", ring(4, 1))
    own_o = swap(own)
    next_m, prev_m = lax.optimization_barrier((next_m, prev_m))
    next_o, prev_o = swap(next_m), swap(prev_m)
    opp_g, own_o = lax.optimization_barrier((opp_g, own_o))
    opp = full_rows(opp_g)
    opp, next_o, prev_o = lax.optimization_barrier((opp, next_o, prev_o))
    pre0 = dot(tok_m, own[:, :HALF]) + dot(tok_o, own_o[:, :HALF])
    slots = [(own, own_o), (next_m, next_o), (opp, swap(opp)), (prev_m, prev_o)]
    flat = [w for pair in slots for w in pair]
    anywhere = pl.BlockSpec(memory_space=pl.ANY)
    in_smem = pl.BlockSpec(memory_space=pltpu.SMEM)
    params = pltpu.CompilerParams(vmem_limit_bytes=VMEM_LIMIT)
    pred_s, pred_d, pre, score, loss = pl.pallas_call(
        forward_kernel,
        out_shape=(
            jax.ShapeDtypeStruct((rows, SAM), F32),
            jax.ShapeDtypeStruct((rows, DINO), F32),
            jax.ShapeDtypeStruct((4, rows, HALF), F32),
            jax.ShapeDtypeStruct((rows, 4), F32),
            jax.ShapeDtypeStruct((16, 1, 128), F32),
        ),
        in_specs=[in_smem] + [in_vmem] * 6 + [anywhere] * 8,
        out_specs=(in_vmem,) * 5,
        scratch_shapes=[
            pltpu.VMEM((4, rows, HALF), BF16),
            pltpu.VMEM((6, HALF, HALF), BF16),
            pltpu.VMEM((2, HALF, DINO), BF16),
            pltpu.VMEM((2, HALF, SAM), BF16),
            pltpu.SemaphoreType.DMA((16,)),
        ],
        compiler_params=params,
        name="forward",
    )(place, tok_m, tok_o, pre0, goal_s, goal_d, live, *flat)

    loss = lax.all_to_all(loss, ("z", "core"), split_axis=0, concat_axis=0, tiled=True)
    hid = pl.pallas_call(
        hidden_kernel,
        out_shape=jax.ShapeDtypeStruct((4, rows, HALF), BF16),
        in_specs=[in_smem] + [in_vmem] * 7 + [anywhere] * 8,
        out_specs=in_vmem,
        scratch_shapes=[
            pltpu.VMEM((2, HALF, DINO), BF16),
            pltpu.VMEM((2, HALF, SAM), BF16),
            pltpu.SemaphoreType.DMA((10,)),
        ],
        compiler_params=params,
        name="hidden",
    )(place, pred_s, pred_d, goal_s, goal_d, score, scale, pre, *flat)

    loss = jnp.broadcast_to(jnp.sum(loss, axis=0, keepdims=True), (32, 1, 128))
    loss, hid = lax.optimization_barrier((loss, hid))
    loss = lax.all_to_all(loss, ("x", "ylo", "yhi"), split_axis=0, concat_axis=0, tiled=True)
    loss = jnp.sum(loss[:, 0, 0]) / count

    grad = pl.pallas_call(
        grad_kernel,
        out_shape=jax.ShapeDtypeStruct((rows, 2 * HALF), BF16),
        in_specs=[in_smem, in_vmem] + [anywhere] * 8,
        out_specs=in_vmem,
        scratch_shapes=[
            pltpu.VMEM((rows, 4 * HALF), BF16),
            pltpu.VMEM((2, HALF, 4 * HALF), BF16),
            pltpu.SemaphoreType.DMA((8,)),
        ],
        compiler_params=params,
        name="grad",
    )(place, hid, *flat)
    return (grad, loss)


def solution(mesh):
    fine = Mesh(mesh.devices.reshape(4, 2, 8, 2, 4), AXES)
    tokens = P(AXES, None)
    rest = ("ylo", "z", "core", "yhi")
    return jax.shard_map(
        shards,
        mesh=fine,
        in_specs=(
            tokens,
            P(None, rest, "x"),
            P(None, rest, "x"),
            P(),
            P(),
            P(),
            P(rest, None),
            P(rest, None),
            P(rest, None),
            P(rest, None),
        ),
        out_specs=(tokens, P()),
        check_vma=False,
    )
```
